256 devices in a mesh: row: 16 (over z, core), col: 16 (over x, y).
Axes of the slice: x: 4, y: 4, z: 8, core: 2. Of those that a mesh axis runs over, the one named last changes fastest.
Arguments:
- tiles: bfloat16 [16, 16, 64, 256, 256], P('row', 'col'), may hold values from -0.21875 to 0.21875
- tile_row: int32 [16, 16, 64], P('row', 'col'), may hold values from 0 to 63
- tile_col: int32 [16, 16, 64], P('row', 'col'), may hold values from 0 to 255
- live_count: int32 [16, 16], P('row', 'col'), may hold values from 16 to 64, as said below
- cost: float32 [1048576], P('col'), may hold values from -6 to 6
- upper: float32 [1048576], P('col'), may hold values from 0.5 to 2
- capacity: float32 [262144], P('row'), may hold values from 0.05 to 0.5
- step_sizes: float32 [2], replicated, may hold values from 0.2 to 0.6
- restart_flags: int32 [4], replicated, may hold values from 0 to 1
Outputs:
- primal: float32 [1048576], P('col')
- dual: float32 [262144], P('row')
- movement: float32 [4], replicated
The draws below stay inside these ranges and needn't reach their ends.
Inputs may be any that keep to these rules, and one draw needn't show every extreme that they name: `live_count`: at least one device uses all 64 slots.
All inputs are finite; a program needn't handle non-finite values.
Results may differ from the reference program's by a relative error of at most 0.0075.
Values sent between devices are 32-bit elements; how exact they have to be, the bound alone decides.
A program may use at most 64 MiB of HBM per device.

```python
import math
import jax
import jax.numpy as jnp
from jax import lax

TILE = 256
RB_DEV = 64
CB_DEV = 256
TILES_DEV = 64
ITERS = 4
ROW_GROUPS = 16
COL_GROUPS = 16
NR = 262144
NV = 1048576
N_COL = 16


def draw_live_count(key, part):
    key = jax.random.fold_in(key, 7)
    first, second = jax.random.split(key)
    counts = jax.random.randint(first, (ROW_GROUPS * COL_GROUPS,), TILES_DEV // 4, TILES_DEV + 1)
    place = jax.random.randint(second, (), 0, ROW_GROUPS * COL_GROUPS)
    counts = counts.at[place].set(TILES_DEV)
    return counts.reshape(ROW_GROUPS, COL_GROUPS).astype(jnp.int32)


def with_ends(array, own_key, low, high):
    dims = array.shape
    index_at = [jax.random.randint(jax.random.fold_in(own_key, axis), (), 0, dims[axis]) for axis in range(len(dims))]
    array = array.at[tuple(index_at)].set(low)
    longest = dims.index(max(dims))
    index_at[longest] = (index_at[longest] + 1) % dims[longest]
    return array.at[tuple(index_at)].set(high)


def levels(own_key, extent, cuts, smallest, top_value):
    gain, own = 1.0, jax.random.fold_in(own_key, 6)
    for axis_at, blocks in cuts:
        steps = jnp.exp(jax.random.uniform(jax.random.fold_in(own, axis_at), (blocks,), jnp.float32, smallest / len(cuts), top_value / len(cuts)))
        gain = gain * jnp.repeat(steps, extent[axis_at] // blocks).reshape([-1 if axis == axis_at else 1 for axis in range(len(extent))])
    return gain


def centred(key, shape, deviation, reach, pieces=(), kind=jnp.bfloat16):
    values = jax.random.normal(key, shape, jnp.float32) * deviation
    if len(pieces) > 0:
        values = levels(key, shape, pieces, -0.22, 0.18) * values
    return jnp.clip(values, min=-reach, max=reach).astype(kind)


def setup_inputs(seed: int = 0) -> dict:
    arg_keys = jax.random.split(jax.random.key(seed), 10)
    tiles = centred(arg_keys[0], (ROW_GROUPS, COL_GROUPS, TILES_DEV, TILE, TILE), (TILE * TILES_DEV * N_COL // (6 * RB_DEV)) ** -0.5, 0.21875, ((0, 16), (1, 16)))
    tile_row = with_ends(jax.random.randint(arg_keys[1], (ROW_GROUPS, COL_GROUPS, TILES_DEV), 0, RB_DEV), jax.random.fold_in(arg_keys[1], 1), 0, RB_DEV - 1).astype(jnp.int32)
    tile_col = with_ends(jax.random.randint(arg_keys[2], (ROW_GROUPS, COL_GROUPS, TILES_DEV), 0, CB_DEV), jax.random.fold_in(arg_keys[2], 1), 0, CB_DEV - 1).astype(jnp.int32)
    live_count = draw_live_count(jax.random.fold_in(arg_keys[9], 71), 0)
    cost = centred(arg_keys[4], (NV,), 1.0, 6.0, ((0, 16),), jnp.float32)
    upper = jnp.clip(0.5 + 1.5 * jax.random.uniform(arg_keys[5], (NV,), jnp.float32) ** levels(arg_keys[5], (NV,), ((0, 16),), -0.2, 0.2), 0.5, 2.0)
    capacity = jnp.clip(0.05 + 0.45 * jax.random.uniform(arg_keys[6], (NR,), jnp.float32) ** levels(arg_keys[6], (NR,), ((0, 16),), -0.2, 0.2), 0.05, 0.5)
    step_sizes = jnp.clip(jnp.exp(jax.random.uniform(arg_keys[7], (2,), jnp.float32, math.log(0.2), math.log(0.6))), 0.2, 0.6)
    restart_flags = with_ends(jax.random.randint(arg_keys[8], (ITERS,), 0, 2), jax.random.fold_in(arg_keys[8], 1), 0, 1).astype(jnp.int32)
    return dict(tiles=tiles, tile_row=tile_row, tile_col=tile_col, live_count=live_count, cost=cost, upper=upper, capacity=capacity, step_sizes=step_sizes, restart_flags=restart_flags)


def device_products(tiles, tile_row, tile_col, live_count, source, forward):
    groups = ROW_GROUPS * COL_GROUPS
    flat_tiles = tiles.reshape(groups, TILES_DEV, TILE, TILE)
    flat_rows = tile_row.reshape(groups, TILES_DEV)
    flat_cols = tile_col.reshape(groups, TILES_DEV)
    flat_live = live_count.reshape(groups)
    places = jnp.arange(groups, dtype=jnp.int32)

    def one_device(item):
        tile_set, rows_idx, cols_idx, count, place = item
        group_r = place // COL_GROUPS
        group_c = place % COL_GROUPS
        live = (jnp.arange(TILES_DEV, dtype=jnp.int32) < count).astype(jnp.float32)
        dense = tile_set.astype(jnp.float32)
        if forward:
            picked = source[group_c][cols_idx].astype(jnp.float32)
            terms = jnp.einsum('tij,tj->ti', dense, picked, precision=lax.Precision.HIGHEST)
            table = (rows_idx[:, None] == jnp.arange(RB_DEV, dtype=jnp.int32)[None, :]).astype(jnp.float32)
        else:
            picked = source[group_r][rows_idx].astype(jnp.float32)
            terms = jnp.einsum('tij,ti->tj', dense, picked, precision=lax.Precision.HIGHEST)
            table = (cols_idx[:, None] == jnp.arange(CB_DEV, dtype=jnp.int32)[None, :]).astype(jnp.float32)
        table = table * live[:, None]
        return jnp.dot(table.T, terms, precision=lax.Precision.HIGHEST)
    result = lax.map(one_device, (flat_tiles, flat_rows, flat_cols, flat_live, places))
    result = result.reshape(ROW_GROUPS, COL_GROUPS, -1, TILE)
    if forward:
        return lax.optimization_barrier(jnp.sum(result, axis=1)).reshape(NR)
    return lax.optimization_barrier(jnp.sum(result, axis=0)).reshape(NV)

def reference(tiles, tile_row, tile_col, live_count, cost, upper, capacity, step_sizes, restart_flags):
    tau = step_sizes[0]
    sigma = step_sizes[1]
    primal = jnp.zeros((NV,), jnp.float32)
    dual = jnp.zeros((NR,), jnp.float32)
    sum_primal = jnp.zeros((NV,), jnp.float32)
    sum_dual = jnp.zeros((NR,), jnp.float32)
    counter = jnp.zeros((), jnp.float32)
    moves = []
    for step in range(ITERS):
        dual_low = dual.astype(jnp.bfloat16).reshape(ROW_GROUPS, RB_DEV, TILE)
        gradient = device_products(tiles, tile_row, tile_col, live_count, dual_low, False)
        primal_new = jnp.clip(primal - tau * (cost + gradient), 0.0, upper)
        extrapolated = (2.0 * primal_new - primal).astype(jnp.bfloat16).reshape(COL_GROUPS, CB_DEV, TILE)
        load = device_products(tiles, tile_row, tile_col, live_count, extrapolated, True)
        dual_new = jnp.maximum(dual + sigma * (load - capacity), 0.0)
        primal_step = primal_new - primal
        dual_step = dual_new - dual
        moves.append(jnp.sqrt(jnp.sum(primal_step * primal_step) / tau + jnp.sum(dual_step * dual_step) / sigma + 1e-06))
        sum_primal = sum_primal + primal_new
        sum_dual = sum_dual + dual_new
        counter = counter + 1.0
        flag = restart_flags[step] == 1
        primal = jnp.where(flag, sum_primal / counter, primal_new)
        dual = jnp.where(flag, sum_dual / counter, dual_new)
        sum_primal = jnp.where(flag, 0.0, sum_primal)
        sum_dual = jnp.where(flag, 0.0, sum_dual)
        counter = jnp.where(flag, 0.0, counter)
    return (primal, dual, jnp.stack(moves))
```

```python
import functools

import jax
import jax.numpy as jnp
from jax import lax
from jax.experimental import pallas as pl
from jax.experimental.pallas import tpu as pltpu
from jax.sharding import PartitionSpec as P

ITERS = 4
LANES = 128
GROUP = 16
MESH = pl.DeviceIdType.MESH


def split_dot(table, values):
    high = values.astype(jnp.bfloat16)
    rest = values - high.astype(jnp.float32)
    mid = rest.astype(jnp.bfloat16)
    low = (rest - mid.astype(jnp.float32)).astype(jnp.bfloat16)
    out = jnp.dot(table, low, preferred_element_type=jnp.float32)
    out += jnp.dot(table, mid, preferred_element_type=jnp.float32)
    return out + jnp.dot(table, high, preferred_element_type=jnp.float32)


def kernel(
    n_row, n_col,
    tiles_hbm, col_ref, row_ref, cost_hbm, upper_hbm, cap_hbm, count_ref, step_ref, flag_ref,
    primal_out, dual_out, move_out,
    tiles, cost, upper, cap, col_table, col_pick, row_table, row_pick,
    primal, sum_primal, dual, sum_dual, picked, terms,
    grad, pair_in, pair_sum, ring_in, primal_new, load, load_in, dual_new,
    primal_sq, dual_sq, primal_sq_in, dual_sq_in,
    tile_sem, in_sem, out_sem,
    pair_send, pair_recv, ring_send, ring_recv, gather_send, gather_recv, half_send, half_recv,
    load_send, load_recv, dual_send, dual_recv, sq_send, sq_recv,
):
    r = lax.axis_index("row")
    c = lax.axis_index("col")
    z, core = lax.div(r, 2), lax.rem(r, 2)
    n_z = n_row // 2
    slots, width = tiles.shape[0], tiles.shape[1]
    p_rows, d_rows = primal.shape[0], dual.shape[0]
    p_half, p_share, d_share = p_rows // 2, p_rows // n_row, d_rows // n_col
    groups = slots // GROUP
    sibling = (2 * z + 1 - core, c)

    def tile_copy(g):
        part = pl.ds(g * GROUP, GROUP)
        return pltpu.make_async_copy(tiles_hbm.at[part], tiles.at[part], tile_sem.at[g])

    for g in range(groups):
        tile_copy(g).start()
    in_copies = [
        pltpu.make_async_copy(src, dst, in_sem.at[i])
        for i, (src, dst) in enumerate(((cost_hbm, cost), (upper_hbm, upper), (cap_hbm, cap)))
    ]
    for copy in in_copies:
        copy.start()

    barrier = pltpu.get_barrier_semaphore()
    for o in range(1, n_row):
        pl.semaphore_signal(barrier, inc=1, device_id=(lax.rem(r + o, n_row), c), device_id_type=MESH)
    for o in range(1, n_col):
        pl.semaphore_signal(barrier, inc=1, device_id=(r, lax.rem(c + o, n_col)), device_id_type=MESH)

    lane = lax.broadcasted_iota(jnp.int32, (1, 2 * slots), 1)
    live = lax.rem(lane, slots) < count_ref[0, 0]

    def tables(index_ref, n_rows, table, pick):
        twice = index_ref[...] * 2
        key = jnp.where(live, jnp.concatenate([twice, twice + 1], axis=1), -1)
        hot = jnp.where(lax.broadcasted_iota(jnp.int32, (n_rows, 2 * slots), 0) == key, 1.0, 0.0)
        table[...] = hot.astype(jnp.bfloat16)
        pick[...] = hot.T.astype(jnp.bfloat16)

    tables(col_ref, p_rows, col_table, col_pick)
    tables(row_ref, d_rows, row_table, row_pick)
    for ref in (primal, sum_primal, dual, sum_dual, primal_sq, dual_sq):
        ref[...] = jnp.zeros_like(ref)
    tau, sigma = step_ref[0], step_ref[1]
    for copy in in_copies:
        copy.wait()
    for g in range(groups):
        tile_copy(g).wait()
    pl.semaphore_wait(barrier, n_row - 1 + n_col - 1)

    def pick_blocks(pick, values):
        both = jnp.dot(pick[...], values.astype(jnp.bfloat16), preferred_element_type=jnp.float32)
        picked[...] = jnp.concatenate([both[:slots], both[slots:]], axis=1).astype(jnp.bfloat16)

    def place_terms(table):
        both = jnp.concatenate([terms[:, :LANES], terms[:, LANES:]], axis=0)
        return split_dot(table[...], both)

    def transposed_product():
        at_row = lax.broadcasted_iota(jnp.int32, (GROUP, GROUP * width), 0)
        at_tile = lax.div(lax.broadcasted_iota(jnp.int32, (GROUP, GROUP * width), 1), width)
        for g in range(groups):
            part = pl.ds(g * GROUP, GROUP)
            wide = jnp.concatenate([picked[part, :]] * GROUP, axis=1)
            left = jnp.where(at_row == at_tile, wide, jnp.zeros((), jnp.bfloat16))
            right = tiles[part].reshape(GROUP * width, width)
            terms[part, :] = jnp.dot(left, right, preferred_element_type=jnp.float32)

    def forward_product():
        at_row = lax.broadcasted_iota(jnp.int32, (GROUP, width), 0)

        def group(g, _):
            part = pl.ds(pl.multiple_of(g * GROUP, GROUP), GROUP)
            mine = picked[part, :]
            total = jnp.zeros((GROUP, width), jnp.float32)
            for s in range(GROUP):
                left = jnp.where(at_row == s, mine, jnp.zeros((), jnp.bfloat16))
                total += lax.dot_general(
                    left, tiles[g * GROUP + s], (((1,), (1,)), ((), ())), preferred_element_type=jnp.float32
                )
            terms[part, :] = total
            return 0

        lax.fori_loop(0, groups, group, 0)

    def p_part(which_core, which_z):
        return pl.ds(pl.multiple_of(which_core * p_half + which_z * p_share, 8), p_share)

    def half_part(which_z):
        return pl.ds(pl.multiple_of(which_z * p_share, 8), p_share)

    def d_part(which):
        return pl.ds(pl.multiple_of(which * d_share, 8), d_share)

    def remote(src, dst, send, recv, device):
        return pltpu.make_async_remote_copy(
            src_ref=src, dst_ref=dst, send_sem=send, recv_sem=recv, device_id=device, device_id_type=MESH
        )

    far_first = sorted(range(1, n_z), key=lambda o: -min(o, n_z - o))
    own_p = p_part(core, z)
    own_d = d_part(c)
    other_core = 1 - core

    def iteration(k, counter):
        pick_blocks(row_pick, dual[...])
        transposed_product()
        grad[k] = place_terms(col_table)
        pair = {}
        for o in far_first + [0]:
            to_z = lax.rem(z + o, n_z)
            pair[o] = remote(
                grad.at[k, p_part(other_core, to_z)], pair_in.at[k, half_part(to_z)],
                pair_send.at[k, o], pair_recv.at[k, o], sibling,
            )
            pair[o].start()
        for o in far_first:
            to_z = lax.rem(z + o, n_z)
            pair[o].wait_recv()
            pair_sum[k, half_part(to_z)] = grad[k, p_part(core, to_z)] + pair_in[k, half_part(to_z)]
            remote(
                pair_sum.at[k, half_part(to_z)], ring_in.at[k, o - 1],
                ring_send.at[k], ring_recv.at[k], (2 * to_z + core, c),
            ).start()
        pair[0].wait_recv()
        gradient = grad[k, own_p] + pair_in[k, half_part(z)]
        whole_ring = remote(ring_in.at[k], ring_in.at[k], ring_send.at[k], ring_recv.at[k], sibling)
        whole_ring.wait_recv()
        for o in range(n_z - 1):
            gradient += ring_in[k, o]

        primal_new[k, own_p] = jnp.clip(primal[own_p] - tau * (cost[own_p] + gradient), 0.0, upper[own_p])
        for o in far_first:
            to_z = lax.rem(z + o, n_z)
            remote(
                primal_new.at[k, own_p], primal_new.at[k, own_p],
                gather_send.at[k], gather_recv.at[k], (2 * to_z + core, c),
            ).start()
        others = primal_new.at[k, pl.ds(0, (n_z - 1) * p_share)]
        whole_gather = remote(others, others, gather_send.at[k], gather_recv.at[k], sibling)
        whole_gather.wait_recv()
        own_half = primal_new.at[k, pl.ds(pl.multiple_of(core * p_half, 8), p_half)]
        half = remote(own_half, own_half, half_send.at[k], half_recv.at[k], sibling)
        half.start()
        half.wait_recv()

        fresh = primal_new[k]
        pick_blocks(col_pick, 2.0 * fresh - primal[...])
        forward_product()
        load[k] = place_terms(row_table)
        for o in range(1, n_col):
            to = lax.rem(c + o, n_col)
            remote(
                load.at[k, d_part(to)], load_in.at[k, o - 1], load_send.at[k], load_recv.at[k], (r, to)
            ).start()

        counter = counter + 1.0
        flag = jnp.where(flag_ref[k] == 1, 1.0, 0.0)
        fresh = primal_new[k]
        step = fresh - primal[...]
        primal_sq[pl.ds(k, 1), :] = jnp.sum(step * step, axis=0, keepdims=True)
        total = sum_primal[...] + fresh
        again = jnp.full((p_rows, LANES), flag) > 0.5
        primal[...] = jnp.where(again, total / jnp.full((p_rows, LANES), counter), fresh)
        sum_primal[...] = jnp.where(again, 0.0, total)

        whole_load = remote(load_in.at[k], load_in.at[k], load_send.at[k], load_recv.at[k], sibling)
        whole_load.wait_recv()
        loaded = load[k, own_d]
        for o in range(n_col - 1):
            loaded += load_in[k, o]
        dual_new[k, own_d] = jnp.maximum(dual[own_d] + sigma * (loaded - cap[own_d]), 0.0)
        for o in range(1, n_col):
            to = lax.rem(c + o, n_col)
            remote(
                dual_new.at[k, own_d], dual_new.at[k, own_d], dual_send.at[k], dual_recv.at[k], (r, to)
            ).start()
        other_d = dual_new.at[k, pl.ds(0, (n_col - 1) * d_share)]
        whole_dual = remote(other_d, other_d, dual_send.at[k], dual_recv.at[k], sibling)
        whole_dual.wait_recv()

        fresh = dual_new[k]
        step = fresh - dual[...]
        dual_sq[pl.ds(k, 1), :] = jnp.sum(step * step, axis=0, keepdims=True)
        total = sum_dual[...] + fresh
        again = jnp.full((d_rows, LANES), flag) > 0.5
        dual[...] = jnp.where(again, total / jnp.full((d_rows, LANES), counter), fresh)
        sum_dual[...] = jnp.where(again, 0.0, total)

        for o in range(n_z):
            pair[o].wait_send()
        whole_ring.wait_send()
        whole_gather.wait_send()
        half.wait_send()
        whole_load.wait_send()
        whole_dual.wait_send()
        return jnp.where(flag_ref[k] == 1, 0.0, counter)

    lax.fori_loop(0, ITERS, iteration, jnp.float32(0.0))

    out_copies = [
        pltpu.make_async_copy(primal, primal_out, out_sem.at[0]),
        pltpu.make_async_copy(dual, dual_out, out_sem.at[1]),
    ]
    for copy in out_copies:
        copy.start()
    for o in range(1, n_row):
        to = lax.rem(r + o, n_row)
        remote(dual_sq, dual_sq_in.at[r], sq_send.at[0], sq_recv.at[0], (to, c)).start()
    for o in range(1, n_col):
        to = lax.rem(c + o, n_col)
        remote(primal_sq, primal_sq_in.at[c], sq_send.at[1], sq_recv.at[1], (r, to)).start()
    dual_sq_in[r] = dual_sq[...]
    primal_sq_in[c] = primal_sq[...]
    for i, (ref, n) in enumerate(((dual_sq_in, n_row), (primal_sq_in, n_col))):
        part = ref.at[pl.ds(0, n - 1)]
        whole = remote(part, part, sq_send.at[i], sq_recv.at[i], sibling)
        whole.wait_recv()
        whole.wait_send()
    p_total = jnp.sum(jnp.sum(primal_sq_in[...], axis=0), axis=1, keepdims=True)
    d_total = jnp.sum(jnp.sum(dual_sq_in[...], axis=0), axis=1, keepdims=True)
    moves = jnp.sqrt(p_total / tau + d_total / sigma + 1e-6)
    for k in range(ITERS):
        move_out[k] = moves[k, 0]
    for copy in out_copies:
        copy.wait()


def shards(n_row, n_col, tiles, tile_row, tile_col, live_count, cost, upper, capacity, step_sizes, restart_flags):
    slots, width = tiles.shape[2], tiles.shape[3]
    p_rows, d_rows = cost.shape[0] // LANES, capacity.shape[0] // LANES
    p_share, d_share, n_z = p_rows // n_row, d_rows // n_col, n_row // 2
    f32, bf16 = jnp.float32, jnp.bfloat16
    vmem, smem, hbm = (pl.BlockSpec(memory_space=m) for m in (pltpu.VMEM, pltpu.SMEM, pl.ANY))
    dma = pltpu.SemaphoreType.DMA
    primal, dual, moves = pl.pallas_call(
        functools.partial(kernel, n_row, n_col),
        out_shape=(
            jax.ShapeDtypeStruct((p_rows, LANES), f32),
            jax.ShapeDtypeStruct((d_rows, LANES), f32),
            jax.ShapeDtypeStruct((ITERS,), f32),
        ),
        in_specs=[hbm, vmem, vmem, hbm, hbm, hbm, smem, smem, smem],
        out_specs=(hbm, hbm, smem),
        scratch_shapes=[
            pltpu.VMEM((slots, width, width), bf16),
            pltpu.VMEM((p_rows, LANES), f32),
            pltpu.VMEM((p_rows, LANES), f32),
            pltpu.VMEM((d_rows, LANES), f32),
            pltpu.VMEM((p_rows, 2 * slots), bf16),
            pltpu.VMEM((2 * slots, p_rows), bf16),
            pltpu.VMEM((d_rows, 2 * slots), bf16),
            pltpu.VMEM((2 * slots, d_rows), bf16),
            pltpu.VMEM((p_rows, LANES), f32),
            pltpu.VMEM((p_rows, LANES), f32),
            pltpu.VMEM((d_rows, LANES), f32),
            pltpu.VMEM((d_rows, LANES), f32),
            pltpu.VMEM((slots, width), bf16),
            pltpu.VMEM((slots, width), f32),
            pltpu.VMEM((ITERS, p_rows, LANES), f32),
            pltpu.VMEM((ITERS, p_rows // 2, LANES), f32),
            pltpu.VMEM((ITERS, p_rows // 2, LANES), f32),
            pltpu.VMEM((ITERS, n_z - 1, p_share, LANES), f32),
            pltpu.VMEM((ITERS, p_rows, LANES), f32),
            pltpu.VMEM((ITERS, d_rows, LANES), f32),
            pltpu.VMEM((ITERS, n_col - 1, d_share, LANES), f32),
            pltpu.VMEM((ITERS, d_rows, LANES), f32),
            pltpu.VMEM((8, LANES), f32),
            pltpu.VMEM((8, LANES), f32),
            pltpu.VMEM((n_col, 8, LANES), f32),
            pltpu.VMEM((n_row, 8, LANES), f32),
            dma((slots // GROUP,)), dma((3,)), dma((2,)),
            dma((ITERS, n_z)), dma((ITERS, n_z)),
            dma((ITERS,)), dma((ITERS,)), dma((ITERS,)), dma((ITERS,)), dma((ITERS,)), dma((ITERS,)),
            dma((ITERS,)), dma((ITERS,)), dma((ITERS,)), dma((ITERS,)), dma((2,)), dma((2,)),
        ],
        compiler_params=pltpu.CompilerParams(
            collective_id=0, has_side_effects=True, vmem_limit_bytes=40 * 2**20
        ),
        name="pdhg",
    )(
        tiles.reshape(slots, width, width),
        tile_col.reshape(1, slots),
        tile_row.reshape(1, slots),
        cost.reshape(p_rows, LANES),
        upper.reshape(p_rows, LANES),
        capacity.reshape(d_rows, LANES),
        live_count,
        step_sizes,
        restart_flags,
    )
    return primal.reshape(-1), dual.reshape(-1), moves


def solution(mesh):
    in_specs = (
        P("row", "col", None, None, None),
        P("row", "col", None),
        P("row", "col", None),
        P("row", "col"),
        P("col"),
        P("col"),
        P("row"),
        P(),
        P(),
    )
    out_specs = (P("col"), P("row"), P())
    body = functools.partial(shards, mesh.shape["row"], mesh.shape["col"])
    return jax.shard_map(body, mesh=mesh, in_specs=in_specs, out_specs=out_specs, check_vma=False)
```

```python
import functools

import jax
import jax.numpy as jnp
from jax import lax
from jax.experimental import pallas as pl
from jax.experimental.pallas import tpu as pltpu
from jax.sharding import PartitionSpec as P

ITERS = 4
LANES = 128
GROUP = 16
VMEM_LIMIT = 48 * 2**20
MESH = pl.DeviceIdType.MESH


def split(values):
    high = values.astype(jnp.bfloat16)
    rest = values - high.astype(jnp.float32)
    mid = rest.astype(jnp.bfloat16)
    low = (rest - mid.astype(jnp.float32)).astype(jnp.bfloat16)
    return jnp.concatenate([high, mid, low], axis=0)


def kernel(
    n_row, n_col,
    tiles_hbm, col_hbm, row_hbm, cost_hbm, upper_hbm, cap_hbm, step_hbm, flag_hbm, count_ref,
    primal_out, dual_out, move_out,
    tiles, tiles_t, cost, upper, cap, col_index, row_index, step_ref, flag_ref,
    col_table, col_pick, row_table, row_pick,
    primal, sum_primal, dual, sum_dual, primal_done, dual_done, picked, terms,
    grad, pair_in, pair_sum, ring_in, primal_new, x_in, y_in,
    primal_sq, dual_sq, primal_sq_in, dual_sq_in,
    tile_sem, in_sem, out_sem,
    pair_send, pair_recv, ring_send, ring_recv, gather_send, gather_recv, pass_send, pass_recv,
    line_send, x_recv, y_recv, sq_send, sq_recv,
):
    r = lax.axis_index("row")
    c = lax.axis_index("col")
    z, core = lax.div(r, 2), lax.rem(r, 2)
    n_z, n_line = n_row // 2, int(n_col**0.5)
    x, y = lax.div(c, n_line), lax.rem(c, n_line)
    slots, width = tiles.shape[0], tiles.shape[1]
    p_rows, d_rows = primal.shape[0], dual.shape[0]
    p_half, p_share, d_half = p_rows // 2, p_rows // n_row, d_rows // 2
    groups = slots // GROUP
    other = 1 - core
    sibling = (2 * z + other, c)

    def tile_copy(g):
        part = pl.ds(g * GROUP, GROUP)
        return pltpu.make_async_copy(tiles_hbm.at[part], tiles.at[part], tile_sem.at[g])

    own_in = pl.ds(pl.multiple_of(z * 2 * p_share, 8), 2 * p_share)
    in_copies = [
        pltpu.make_async_copy(src, dst, in_sem.at[i])
        for i, (src, dst) in enumerate((
            (col_hbm, col_index), (row_hbm, row_index), (step_hbm, step_ref),
            (flag_hbm, flag_ref), (cost_hbm.at[own_in], cost), (upper_hbm.at[own_in], upper), (cap_hbm, cap),
        ))
    ]
    for copy in in_copies:
        copy.start()
    for g in range(groups):
        tile_copy(g).start()

    barrier = pltpu.get_barrier_semaphore()
    for o in range(1, n_row):
        pl.semaphore_signal(barrier, inc=1, device_id=(lax.rem(r + o, n_row), c), device_id_type=MESH)
    for o in range(1, n_col):
        pl.semaphore_signal(barrier, inc=1, device_id=(r, lax.rem(c + o, n_col)), device_id_type=MESH)

    for ref in (primal, sum_primal, dual, sum_dual, primal_sq, dual_sq):
        ref[...] = jnp.zeros_like(ref)
    for copy in in_copies:
        copy.wait()

    lane = lax.broadcasted_iota(jnp.int32, (1, 3 * slots), 1)
    live = lax.rem(lane, slots) < count_ref[0, 0]

    def tables(index_ref, n_blocks, table, pick):
        index = index_ref[...]
        key = jnp.where(live, jnp.concatenate([index, index, index], axis=1), -1)
        hot = jnp.where(lax.broadcasted_iota(jnp.int32, (n_blocks, 3 * slots), 0) == key, 1.0, 0.0)
        table[...] = hot.astype(jnp.bfloat16)
        pick[...] = hot[:, :slots].T.astype(jnp.bfloat16)

    tables(row_index, d_half, row_table, row_pick)
    tables(col_index, p_half, col_table, col_pick)
    tau, sigma = step_ref[0], step_ref[1]

    def deal(ref, rows):
        return ref[pl.ds(0, rows, stride=2), :], ref[pl.ds(1, rows, stride=2), :]

    def weave(ref, out):
        rows = ref.shape[0] // 2
        out[pl.ds(0, rows, stride=2), :] = ref[:rows]
        out[pl.ds(1, rows, stride=2), :] = ref[rows:]

    first = jnp.full((p_share, LANES), core) == 0
    own_cost = jnp.where(first, *deal(cost, p_share))
    own_upper = jnp.where(first, *deal(upper, p_share))
    capacity = jnp.concatenate(deal(cap, d_half), axis=0)
    for g in range(groups):
        tile_copy(g).wait()

    def half_lanes(h):
        return pl.ds(pl.multiple_of(h * LANES, LANES), LANES)

    def pick_blocks(pick, values, h):
        chosen = jnp.dot(pick[...], values.astype(jnp.bfloat16), preferred_element_type=jnp.float32)
        picked[:, half_lanes(h)] = chosen.astype(jnp.bfloat16)

    def diagonal(values):
        depth = values.shape[1]
        at_row = lax.broadcasted_iota(jnp.int32, (GROUP, GROUP * depth), 0)
        at_tile = lax.div(lax.broadcasted_iota(jnp.int32, (GROUP, GROUP * depth), 1), depth)
        wide = jnp.concatenate([values] * GROUP, axis=1)
        return jnp.where(at_row == at_tile, wide, jnp.zeros((), jnp.bfloat16))

    def group_part(g):
        return pl.ds(g * GROUP, GROUP)

    def transposed_half(h):
        for g in range(groups):
            part = group_part(g)
            right = tiles[part, :, half_lanes(h)].reshape(GROUP * width, LANES)
            terms[part, :LANES] = jnp.dot(diagonal(picked[part, :]), right, preferred_element_type=jnp.float32)
        return jnp.dot(col_table[...], split(terms[:, :LANES]), preferred_element_type=jnp.float32)

    def forward_half(h, add):
        depth = pl.ds(pl.multiple_of(h * LANES, LANES), LANES)
        for g in range(groups):
            part = group_part(g)
            right = tiles_t[part, depth, :].reshape(GROUP * LANES, width)
            some = jnp.dot(diagonal(picked[part, half_lanes(h)]), right, preferred_element_type=jnp.float32)
            terms[part, :] = terms[part, :] + some if add else some

    def transpose_tiles():
        def four(i, _):
            for s in range(4):
                tiles_t[4 * i + s] = tiles[4 * i + s].T
            return 0

        lax.fori_loop(0, slots // 4, four, 0)

    def half_part(h):
        return pl.ds(pl.multiple_of(h * p_half, 8), p_half)

    def z_part(which_z):
        return pl.ds(pl.multiple_of(which_z * p_share, 8), p_share)

    def p_part(h, which_z):
        return pl.ds(pl.multiple_of(h * p_half + which_z * p_share, 8), p_share)

    def remote(src, dst, send, recv, device):
        return pltpu.make_async_remote_copy(
            src_ref=src, dst_ref=dst, send_sem=send, recv_sem=recv, device_id=device, device_id_type=MESH
        )

    def at_z(o):
        return (2 * lax.rem(z + o, n_z) + core, c)

    near_first = sorted(range(1, n_z), key=lambda o: min(o, n_z - o))
    far_first = near_first[::-1]
    own_p = p_part(core, z)
    x_peers = [(r, lax.rem(x + o, n_line) * n_line + y) for o in range(1, n_line)]
    y_peers = [(r, x * n_line + lax.rem(y + o, n_line)) for o in range(1, n_line)]

    def sum_lines(ref, k, phase):
        total = ref[k, phase, 0]
        for i in range(1, n_line):
            total += ref[k, phase, i]
        return total

    def start_x(k, phase):
        for peer in x_peers:
            remote(x_in.at[k, phase, x], x_in.at[k, phase, x], line_send.at[k], x_recv.at[k, phase], peer).start()

    def start_y(k, phase):
        for peer in y_peers:
            remote(y_in.at[k, phase, y], y_in.at[k, phase, y], line_send.at[k], y_recv.at[k, phase], peer).start()

    def wait_line(ref, sem, k, phase):
        part = ref.at[k, phase, pl.ds(0, n_line - 1)]
        remote(part, part, line_send.at[k], sem.at[k, phase], sibling).wait_recv()

    def send_squares(ref, ref_in, i, me, n, device):
        ref_in[me] = ref[...]
        for o in range(1, n):
            to = lax.rem(me + o, n)
            remote(ref, ref_in.at[me], sq_send.at[i], sq_recv.at[i], device(to)).start()

    def gradient_step(k):
        for h in range(2):
            pick_blocks(row_pick, dual[h * d_half:(h + 1) * d_half], h)
        grad[k, half_part(other)] = transposed_half(other)

        @pl.when(k == 0)
        def _():
            pl.semaphore_wait(barrier, n_row - 1 + n_col - 1)

        pair = {}
        for o in far_first + [0]:
            to_z = lax.rem(z + o, n_z)
            pair[o] = remote(
                grad.at[k, p_part(other, to_z)], pair_in.at[k, z_part(to_z)],
                pair_send.at[k], pair_recv.at[k, o], sibling,
            )
            pair[o].start()
        grad[k, half_part(core)] = transposed_half(core)
        for o in far_first:
            to_z = lax.rem(z + o, n_z)
            pair[o].wait_recv()
            pair_sum[k, z_part(to_z)] = grad[k, p_part(core, to_z)] + pair_in[k, z_part(to_z)]
            remote(
                pair_sum.at[k, z_part(to_z)], ring_in.at[k, o - 1], ring_send.at[k], ring_recv.at[k], at_z(o)
            ).start()
        pair[0].wait_recv()
        gradient = grad[k, own_p] + pair_in[k, z_part(z)]

        @pl.when(k == 0)
        def _():
            transpose_tiles()

        remote(ring_in.at[k], ring_in.at[k], ring_send.at[k], ring_recv.at[k], sibling).wait_recv()
        for i in range(n_z - 1):
            gradient += ring_in[k, i]

        primal_new[k, own_p] = jnp.clip(primal[own_p] - tau * (own_cost + gradient), 0.0, own_upper)
        mine = primal_new.at[k, own_p]
        for o in far_first:
            remote(mine, mine, gather_send.at[k], gather_recv.at[k, o], at_z(o)).start()
        remote(mine, mine, pass_send.at[k], pass_recv.at[k], sibling).start()
        for o in near_first:
            here = primal_new.at[k, p_part(core, lax.rem(z + n_z - o, n_z))]
            remote(here, here, gather_send.at[k], gather_recv.at[k, o], sibling).wait_recv()
            remote(here, here, pass_send.at[k], pass_recv.at[k], sibling).start()

    def extrapolated(k, h):
        return 2.0 * primal_new[k, half_part(h)] - primal[half_part(h)]

    def load_step(k, counter):
        pick_blocks(col_pick, extrapolated(k, core), core)
        forward_half(core, False)
        passed = primal_new.at[k, half_part(core)]
        remote(passed, passed, pass_send.at[k], pass_recv.at[k], sibling).wait_recv()
        pick_blocks(col_pick, extrapolated(k, other), other)
        forward_half(other, True)

        x_in[k, 0, x] = jnp.dot(row_table[...], split(terms[:, :LANES]), preferred_element_type=jnp.float32)
        start_x(k, 0)
        y_in[k, 0, y] = jnp.dot(row_table[...], split(terms[:, LANES:]), preferred_element_type=jnp.float32)
        start_y(k, 0)

        counter = counter + 1.0
        flag = jnp.where(flag_ref[k] == 1, 1.0, 0.0)
        fresh = primal_new[k]
        step = fresh - primal[...]
        primal_sq[pl.ds(k, 1), :] = jnp.sum(step * step, axis=0, keepdims=True)
        total = sum_primal[...] + fresh
        again = jnp.full((p_rows, LANES), flag) > 0.5
        primal[...] = jnp.where(again, total / jnp.full((p_rows, LANES), counter), fresh)
        sum_primal[...] = jnp.where(again, 0.0, total)

        wait_line(x_in, x_recv, k, 0)
        y_in[k, 1, y] = sum_lines(x_in, k, 0)
        start_y(k, 1)
        wait_line(y_in, y_recv, k, 0)
        x_in[k, 1, x] = sum_lines(y_in, k, 0)
        start_x(k, 1)

        @pl.when(k == ITERS - 1)
        def _():
            send_squares(primal_sq, primal_sq_in, 1, c, n_col, lambda to: (r, to))
            weave(primal, primal_done)
            pltpu.make_async_copy(primal_done, primal_out, out_sem.at[0]).start()

        wait_line(y_in, y_recv, k, 1)
        wait_line(x_in, x_recv, k, 1)
        loaded = jnp.concatenate([sum_lines(y_in, k, 1), sum_lines(x_in, k, 1)], axis=0)
        old = dual[...]
        fresh = jnp.maximum(old + sigma * (loaded - capacity), 0.0)
        step = fresh - old
        dual_sq[pl.ds(k, 1), :] = jnp.sum(step * step, axis=0, keepdims=True)
        total = sum_dual[...] + fresh
        again = jnp.full((d_rows, LANES), flag) > 0.5
        dual[...] = jnp.where(again, total / jnp.full((d_rows, LANES), counter), fresh)
        sum_dual[...] = jnp.where(again, 0.0, total)
        return jnp.where(flag_ref[k] == 1, 0.0, counter)

    def iteration(k, counter):
        gradient_step(k)
        return load_step(k, counter)

    lax.fori_loop(0, ITERS, iteration, jnp.float32(0.0))

    send_squares(dual_sq, dual_sq_in, 0, r, n_row, lambda to: (to, c))
    weave(dual, dual_done)
    dual_copy = pltpu.make_async_copy(dual_done, dual_out, out_sem.at[1])
    dual_copy.start()

    def sent(k, _):
        def wait(ref, sem):
            remote(ref, ref, sem.at[k], sem.at[k], sibling).wait_send()

        wait(grad.at[k, pl.ds(0, n_z * p_share)], pair_send)
        wait(grad.at[k, pl.ds(0, (n_z - 1) * p_share)], ring_send)
        wait(grad.at[k, pl.ds(0, (n_z - 1) * p_share)], gather_send)
        wait(grad.at[k, pl.ds(0, n_z * p_share)], pass_send)
        for _ in range(2):
            wait(x_in.at[k, 0, pl.ds(0, n_line - 1)], line_send)
            wait(y_in.at[k, 0, pl.ds(0, n_line - 1)], line_send)
        return 0

    lax.fori_loop(0, ITERS, sent, 0)
    for i, (ref, n) in enumerate(((dual_sq_in, n_row), (primal_sq_in, n_col))):
        part = ref.at[pl.ds(0, n - 1)]
        whole = remote(part, part, sq_send.at[i], sq_recv.at[i], sibling)
        whole.wait_send()
        whole.wait_recv()
    p_total = jnp.sum(jnp.sum(primal_sq_in[...], axis=0), axis=1, keepdims=True)
    d_total = jnp.sum(jnp.sum(dual_sq_in[...], axis=0), axis=1, keepdims=True)
    moves = jnp.sqrt(p_total / tau + d_total / sigma + 1e-6)
    for k in range(ITERS):
        move_out[k] = moves[k, 0]
    pltpu.make_async_copy(primal_done, primal_out, out_sem.at[0]).wait()
    dual_copy.wait()


def shards(n_row, n_col, tiles, tile_row, tile_col, live_count, cost, upper, capacity, step_sizes, restart_flags):
    slots, width = tiles.shape[2], tiles.shape[3]
    p_rows, d_rows = cost.shape[0] // LANES, capacity.shape[0] // LANES
    p_share, n_z, n_line = p_rows // n_row, n_row // 2, int(n_col**0.5)
    f32, bf16, i32 = jnp.float32, jnp.bfloat16, jnp.int32
    hbm = pl.BlockSpec(memory_space=pltpu.HBM)
    anywhere = pl.BlockSpec(memory_space=pl.ANY)
    smem = pl.BlockSpec(memory_space=pltpu.SMEM)
    dma = pltpu.SemaphoreType.DMA
    out_shape = (
        jax.ShapeDtypeStruct((p_rows, LANES), f32),
        jax.ShapeDtypeStruct((d_rows, LANES), f32),
        jax.ShapeDtypeStruct((ITERS,), f32),
    )
    primal, dual, moves = pl.pallas_call(
        functools.partial(kernel, n_row, n_col),
        out_shape=out_shape,
        in_specs=[hbm] * 8 + [smem],
        out_specs=(anywhere, anywhere, smem),
        scratch_shapes=[
            pltpu.VMEM((slots, width, width), bf16),
            pltpu.VMEM((slots, width, width), bf16),
            pltpu.VMEM((2 * p_share, LANES), f32),
            pltpu.VMEM((2 * p_share, LANES), f32),
            pltpu.VMEM((d_rows, LANES), f32),
            pltpu.VMEM((1, slots), i32),
            pltpu.VMEM((1, slots), i32),
            pltpu.SMEM((2,), f32),
            pltpu.SMEM((ITERS,), i32),
            pltpu.VMEM((p_rows // 2, 3 * slots), bf16),
            pltpu.VMEM((slots, p_rows // 2), bf16),
            pltpu.VMEM((d_rows // 2, 3 * slots), bf16),
            pltpu.VMEM((slots, d_rows // 2), bf16),
            pltpu.VMEM((p_rows, LANES), f32),
            pltpu.VMEM((p_rows, LANES), f32),
            pltpu.VMEM((d_rows, LANES), f32),
            pltpu.VMEM((d_rows, LANES), f32),
            pltpu.VMEM((p_rows, LANES), f32),
            pltpu.VMEM((d_rows, LANES), f32),
            pltpu.VMEM((slots, width), bf16),
            pltpu.VMEM((slots, width), f32),
            pltpu.VMEM((ITERS, p_rows, LANES), f32),
            pltpu.VMEM((ITERS, p_rows // 2, LANES), f32),
            pltpu.VMEM((ITERS, p_rows // 2, LANES), f32),
            pltpu.VMEM((ITERS, n_z - 1, p_share, LANES), f32),
            pltpu.VMEM((ITERS, p_rows, LANES), f32),
            pltpu.VMEM((ITERS, 2, n_line, d_rows // 2, LANES), f32),
            pltpu.VMEM((ITERS, 2, n_line, d_rows // 2, LANES), f32),
            pltpu.VMEM((8, LANES), f32),
            pltpu.VMEM((8, LANES), f32),
            pltpu.VMEM((n_col, 8, LANES), f32),
            pltpu.VMEM((n_row, 8, LANES), f32),
            dma((slots // GROUP,)), dma((7,)), dma((2,)),
            dma((ITERS,)), dma((ITERS, n_z)), dma((ITERS,)), dma((ITERS,)),
            dma((ITERS,)), dma((ITERS, n_z)), dma((ITERS,)), dma((ITERS,)),
            dma((ITERS,)), dma((ITERS, 2)), dma((ITERS, 2)), dma((2,)), dma((2,)),
        ],
        compiler_params=pltpu.CompilerParams(
            collective_id=0, has_side_effects=True, vmem_limit_bytes=VMEM_LIMIT
        ),
        name="pdhg",
    )(
        *(
            pltpu.with_memory_space_constraint(operand, pltpu.HBM)
            for operand in (
                tiles.reshape(slots, width, width),
                tile_col.reshape(1, slots),
                tile_row.reshape(1, slots),
                cost.reshape(p_rows, LANES),
                upper.reshape(p_rows, LANES),
                capacity.reshape(d_rows, LANES),
                step_sizes,
                restart_flags,
            )
        ),
        live_count,
    )
    return primal.reshape(-1), dual.reshape(-1), moves


def solution(mesh):
    in_specs = (
        P("row", "col", None, None, None),
        P("row", "col", None),
        P("row", "col", None),
        P("row", "col"),
        P("col"),
        P("col"),
        P("row"),
        P(),
        P(),
    )
    out_specs = (P("col"), P("row"), P())
    body = functools.partial(shards, mesh.shape["row"], mesh.shape["col"])
    return jax.shard_map(body, mesh=mesh, in_specs=in_specs, out_specs=out_specs, check_vma=False)
```

```python
import functools

import jax
import jax.numpy as jnp
from jax import lax
from jax.experimental import pallas as pl
from jax.experimental.pallas import tpu as pltpu
from jax.sharding import PartitionSpec as P

ITERS = 4
LANES = 128
GROUP = 16
VMEM_LIMIT = 48 * 2**20
MESH = pl.DeviceIdType.MESH


def split(values):
    high = values.astype(jnp.bfloat16)
    rest = values - high.astype(jnp.float32)
    mid = rest.astype(jnp.bfloat16)
    low = (rest - mid.astype(jnp.float32)).astype(jnp.bfloat16)
    return jnp.concatenate([high, mid, low], axis=0)


def kernel(
    n_row, n_col,
    tiles_hbm, col_hbm, row_hbm, cost_hbm, upper_hbm, cap_hbm, step_hbm, flag_hbm, count_ref,
    primal_out, dual_out, move_out,
    tiles, tiles_t, cost_in, upper_in, cost, upper, cap, col_index, row_index, step_ref, flag_ref,
    col_table, col_pick, row_table, row_pick,
    primal, sum_primal, dual, sum_dual, primal_done, dual_done, picked, terms,
    grad, pair_in, pair_sum, ring_in, primal_new, x_in, y_in,
    primal_sq, dual_sq, primal_sq_in, dual_sq_in,
    tile_sem, in_sem, out_sem,
    pair_send, pair_recv, ring_send, ring_recv, gather_send, gather_recv, pass_send, pass_recv,
    line_send, x_recv, y_recv, sq_send, sq_recv,
):
    r = lax.axis_index("row")
    c = lax.axis_index("col")
    z, core = lax.div(r, 2), lax.rem(r, 2)
    n_z, n_line = n_row // 2, int(n_col**0.5)
    x, y = lax.div(c, n_line), lax.rem(c, n_line)
    slots, width = tiles.shape[0], tiles.shape[1]
    p_rows, d_rows = primal.shape[0], dual.shape[0]
    p_half, p_share, d_half = p_rows // 2, p_rows // n_row, d_rows // 2
    groups = slots // GROUP
    other = 1 - core
    sibling = (2 * z + other, c)

    def tile_copy(g):
        part = pl.ds(g * GROUP, GROUP)
        return pltpu.make_async_copy(tiles_hbm.at[part], tiles.at[part], tile_sem.at[g])

    in_copies = [
        pltpu.make_async_copy(src, dst, in_sem.at[i])
        for i, (src, dst) in enumerate((
            (col_hbm, col_index), (row_hbm, row_index), (step_hbm, step_ref),
            (flag_hbm, flag_ref), (cost_hbm, cost_in), (upper_hbm, upper_in), (cap_hbm, cap),
        ))
    ]
    for copy in in_copies:
        copy.start()
    for g in range(groups):
        tile_copy(g).start()

    barrier = pltpu.get_barrier_semaphore()
    for o in sorted(range(1, n_row), key=lambda o: -min(o, n_row - o)):
        pl.semaphore_signal(barrier, inc=1, device_id=(lax.rem(r + o, n_row), c), device_id_type=MESH)
    for o in range(1, n_col):
        pl.semaphore_signal(barrier, inc=1, device_id=(r, lax.rem(c + o, n_col)), device_id_type=MESH)

    for ref in (primal_sq, dual_sq):
        ref[...] = jnp.zeros_like(ref)
    for copy in in_copies:
        copy.wait()

    lane = lax.broadcasted_iota(jnp.int32, (1, 3 * slots), 1)
    live = lax.rem(lane, slots) < count_ref[0, 0]

    def tables(index_ref, n_blocks, table, pick):
        index = index_ref[...]
        key = jnp.where(live, jnp.concatenate([index, index, index], axis=1), -1)
        hot = jnp.where(lax.broadcasted_iota(jnp.int32, (n_blocks, 3 * slots), 0) == key, 1.0, 0.0)
        table[...] = hot.astype(jnp.bfloat16)
        pick[...] = hot[:, :slots].T.astype(jnp.bfloat16)

    tables(row_index, d_half, row_table, row_pick)
    tables(col_index, p_half, col_table, col_pick)
    tau, sigma = step_ref[0], step_ref[1]

    def deal(ref, rows):
        return ref[pl.ds(0, rows, stride=2), :], ref[pl.ds(1, rows, stride=2), :]

    def weave(ref, out):
        rows = ref.shape[0] // 2
        out[pl.ds(0, rows, stride=2), :] = ref[:rows]
        out[pl.ds(1, rows, stride=2), :] = ref[rows:]

    for dealt, ref in ((cost, cost_in), (upper, upper_in)):
        dealt[:p_half], dealt[p_half:] = deal(ref, p_half)
    capacity = jnp.concatenate(deal(cap, d_half), axis=0)

    def half_lanes(h):
        return pl.ds(pl.multiple_of(h * LANES, LANES), LANES)

    def pick_blocks(pick, values, h):
        chosen = jnp.dot(pick[...], values.astype(jnp.bfloat16), preferred_element_type=jnp.float32)
        picked[:, half_lanes(h)] = chosen.astype(jnp.bfloat16)

    def diagonal(values):
        depth = values.shape[1]
        at_row = lax.broadcasted_iota(jnp.int32, (GROUP, GROUP * depth), 0)
        at_tile = lax.div(lax.broadcasted_iota(jnp.int32, (GROUP, GROUP * depth), 1), depth)
        wide = jnp.concatenate([values] * GROUP, axis=1)
        return jnp.where(at_row == at_tile, wide, jnp.zeros((), jnp.bfloat16))

    def group_part(g):
        return pl.ds(g * GROUP, GROUP)

    def transposed_half(h):
        some = []
        for g in range(groups):
            part = group_part(g)
            right = tiles[part, :, half_lanes(h)].reshape(GROUP * width, LANES)
            some.append(jnp.dot(diagonal(picked[part, :]), right, preferred_element_type=jnp.float32))
        return jnp.dot(col_table[...], split(jnp.concatenate(some, axis=0)), preferred_element_type=jnp.float32)

    def forward_half(h, add):
        depth = pl.ds(pl.multiple_of(h * LANES, LANES), LANES)
        for g in range(groups):
            part = group_part(g)
            right = tiles_t[part, depth, :].reshape(GROUP * LANES, width)
            some = jnp.dot(diagonal(picked[part, half_lanes(h)]), right, preferred_element_type=jnp.float32)
            terms[part, :] = terms[part, :] + some if add else some

    def forward_early():
        at_row = lax.broadcasted_iota(jnp.int32, (GROUP, width), 0)
        for g in range(groups):
            tile_copy(g).wait()
            part = group_part(g)
            mine = picked[part, :]
            total = jnp.zeros((GROUP, width), jnp.float32)
            for s in range(GROUP):
                left = jnp.where(at_row == s, mine, jnp.zeros((), jnp.bfloat16))
                total += lax.dot_general(
                    left, tiles[g * GROUP + s], (((1,), (1,)), ((), ())), preferred_element_type=jnp.float32
                )
            terms[part, :] = total

    def transpose_tiles(begin, end):
        def four(i, _):
            for s in range(4):
                tiles_t[4 * i + s] = tiles[4 * i + s].T
            return 0

        lax.fori_loop(begin // 4, end // 4, four, 0)

    def half_part(h):
        return pl.ds(pl.multiple_of(h * p_half, 8), p_half)

    def z_part(which_z):
        return pl.ds(pl.multiple_of(which_z * p_share, 8), p_share)

    def p_part(h, which_z):
        return pl.ds(pl.multiple_of(h * p_half + which_z * p_share, 8), p_share)

    def remote(src, dst, send, recv, device):
        return pltpu.make_async_remote_copy(
            src_ref=src, dst_ref=dst, send_sem=send, recv_sem=recv, device_id=device, device_id_type=MESH
        )

    def at_z(o):
        return (2 * lax.rem(z + o, n_z) + core, c)

    near_first = sorted(range(1, n_z), key=lambda o: min(o, n_z - o))
    far_first = near_first[::-1]
    own_p = p_part(core, z)
    far_on_line = sorted(range(1, n_line), key=lambda o: -min(o, n_line - o))
    x_peers = [(r, lax.rem(x + o, n_line) * n_line + y) for o in far_on_line]
    y_peers = [(r, x * n_line + lax.rem(y + o, n_line)) for o in far_on_line]

    def sum_lines(ref, k, phase):
        total = ref[k, phase, 0]
        for i in range(1, n_line):
            total += ref[k, phase, i]
        return total

    def start_x(k, phase):
        for peer in x_peers:
            remote(x_in.at[k, phase, x], x_in.at[k, phase, x], line_send.at[k], x_recv.at[k, phase], peer).start()

    def start_y(k, phase):
        for peer in y_peers:
            remote(y_in.at[k, phase, y], y_in.at[k, phase, y], line_send.at[k], y_recv.at[k, phase], peer).start()

    def wait_line(ref, sem, k, phase):
        part = ref.at[k, phase, pl.ds(0, n_line - 1)]
        remote(part, part, line_send.at[k], sem.at[k, phase], sibling).wait_recv()

    def send_squares(ref, ref_in, i, me, n, device):
        ref_in[me] = ref[...]
        for o in sorted(range(1, n), key=lambda o: -min(o, n - o)):
            to = lax.rem(me + o, n)
            remote(ref, ref_in.at[me], sq_send.at[i], sq_recv.at[i], device(to)).start()

    def gradient_step(k):
        for h in range(2):
            pick_blocks(row_pick, dual[h * d_half:(h + 1) * d_half], h)
        grad[k, half_part(other)] = transposed_half(other)
        pair = {}
        for o in far_first + [0]:
            to_z = lax.rem(z + o, n_z)
            pair[o] = remote(
                grad.at[k, p_part(other, to_z)], pair_in.at[k, z_part(to_z)],
                pair_send.at[k], pair_recv.at[k, o], sibling,
            )
            pair[o].start()
        grad[k, half_part(core)] = transposed_half(core)
        for o in far_first:
            to_z = lax.rem(z + o, n_z)
            pair[o].wait_recv()
            pair_sum[k, z_part(to_z)] = grad[k, p_part(core, to_z)] + pair_in[k, z_part(to_z)]
            remote(
                pair_sum.at[k, z_part(to_z)], ring_in.at[k, o - 1], ring_send.at[k], ring_recv.at[k], at_z(o)
            ).start()
        pair[0].wait_recv()
        gradient = grad[k, own_p] + pair_in[k, z_part(z)]
        remote(ring_in.at[k], ring_in.at[k], ring_send.at[k], ring_recv.at[k], sibling).wait_recv()
        for i in range(n_z - 1):
            gradient += ring_in[k, i]

        primal_new[k, own_p] = jnp.clip(primal[own_p] - tau * (cost[own_p] + gradient), 0.0, upper[own_p])
        mine = primal_new.at[k, own_p]
        for o in far_first:
            remote(mine, mine, gather_send.at[k], gather_recv.at[k, o], at_z(o)).start()
        remote(mine, mine, pass_send.at[k], pass_recv.at[k], sibling).start()
        for o in near_first:
            here = primal_new.at[k, p_part(core, lax.rem(z + n_z - o, n_z))]
            remote(here, here, gather_send.at[k], gather_recv.at[k, o], sibling).wait_recv()
            remote(here, here, pass_send.at[k], pass_recv.at[k], sibling).start()

    def extrapolated(k, h):
        return 2.0 * primal_new[k, half_part(h)] - primal[half_part(h)]

    def forward(k):
        pick_blocks(col_pick, extrapolated(k, core), core)
        forward_half(core, False)
        passed = primal_new.at[k, half_part(core)]
        remote(passed, passed, pass_send.at[k], pass_recv.at[k], sibling).wait_recv()
        pick_blocks(col_pick, extrapolated(k, other), other)
        forward_half(other, True)

    def load_step(k, counter, begin):
        x_in[k, 0, x] = jnp.dot(row_table[...], split(terms[:, :LANES]), preferred_element_type=jnp.float32)
        start_x(k, 0)
        y_in[k, 0, y] = jnp.dot(row_table[...], split(terms[:, LANES:]), preferred_element_type=jnp.float32)
        start_y(k, 0)

        counter = counter + 1.0
        flag = jnp.where(flag_ref[k] == 1, 1.0, 0.0)
        fresh = primal_new[k]
        step = fresh - primal[...]
        if begin:
            transpose_tiles(0, slots // 2)
        primal_sq[pl.ds(k, 1), :] = jnp.sum(step * step, axis=0, keepdims=True)
        total = sum_primal[...] + fresh
        again = jnp.full((p_rows, LANES), flag) > 0.5
        primal[...] = jnp.where(again, total / jnp.full((p_rows, LANES), counter), fresh)
        sum_primal[...] = jnp.where(again, 0.0, total)

        wait_line(x_in, x_recv, k, 0)
        y_in[k, 1, y] = sum_lines(x_in, k, 0)
        start_y(k, 1)
        wait_line(y_in, y_recv, k, 0)
        x_in[k, 1, x] = sum_lines(y_in, k, 0)
        start_x(k, 1)
        if begin:
            transpose_tiles(slots // 2, slots)

        @pl.when(k == ITERS - 1)
        def _():
            send_squares(primal_sq, primal_sq_in, 1, c, n_col, lambda to: (r, to))
            weave(primal, primal_done)
            pltpu.make_async_copy(primal_done, primal_out, out_sem.at[0]).start()

        wait_line(y_in, y_recv, k, 1)
        wait_line(x_in, x_recv, k, 1)
        loaded = jnp.concatenate([sum_lines(y_in, k, 1), sum_lines(x_in, k, 1)], axis=0)
        old = dual[...]
        fresh = jnp.maximum(old + sigma * (loaded - capacity), 0.0)
        step = fresh - old
        dual_sq[pl.ds(k, 1), :] = jnp.sum(step * step, axis=0, keepdims=True)
        total = sum_dual[...] + fresh
        again = jnp.full((d_rows, LANES), flag) > 0.5
        dual[...] = jnp.where(again, total / jnp.full((d_rows, LANES), counter), fresh)
        sum_dual[...] = jnp.where(again, 0.0, total)
        return jnp.where(flag_ref[k] == 1, 0.0, counter)

    for ref in (primal, sum_primal, dual, sum_dual):
        ref[...] = jnp.zeros_like(ref)
    gradient_at_zero = 0.0
    primal_new[0] = jnp.clip(primal[...] - tau * (cost[...] + gradient_at_zero), 0.0, upper[...])
    for h in range(2):
        pick_blocks(col_pick, extrapolated(0, h), h)
    forward_early()
    pl.semaphore_wait(barrier, n_row - 1 + n_col - 1)
    counter = load_step(0, jnp.float32(0.0), True)

    def iteration(k, counter):
        gradient_step(k)
        forward(k)
        return load_step(k, counter, False)

    lax.fori_loop(1, ITERS, iteration, counter)

    send_squares(dual_sq, dual_sq_in, 0, r, n_row, lambda to: (to, c))
    weave(dual, dual_done)
    dual_copy = pltpu.make_async_copy(dual_done, dual_out, out_sem.at[1])
    dual_copy.start()

    def sent(k, _, begin=False):
        def wait(ref, sem):
            remote(ref, ref, sem.at[k], sem.at[k], sibling).wait_send()

        for _ in range(2):
            wait(x_in.at[k, 0, pl.ds(0, n_line - 1)], line_send)
            wait(y_in.at[k, 0, pl.ds(0, n_line - 1)], line_send)
        if begin:
            return 0
        wait(grad.at[k, pl.ds(0, n_z * p_share)], pair_send)
        wait(grad.at[k, pl.ds(0, (n_z - 1) * p_share)], ring_send)
        wait(grad.at[k, pl.ds(0, (n_z - 1) * p_share)], gather_send)
        wait(grad.at[k, pl.ds(0, n_z * p_share)], pass_send)
        return 0

    sent(0, 0, True)
    lax.fori_loop(1, ITERS, sent, 0)
    for i, (ref, n) in enumerate(((dual_sq_in, n_row), (primal_sq_in, n_col))):
        part = ref.at[pl.ds(0, n - 1)]
        whole = remote(part, part, sq_send.at[i], sq_recv.at[i], sibling)
        whole.wait_send()
        whole.wait_recv()
    p_total = jnp.sum(jnp.sum(primal_sq_in[...], axis=0), axis=1, keepdims=True)
    d_total = jnp.sum(jnp.sum(dual_sq_in[...], axis=0), axis=1, keepdims=True)
    moves = jnp.sqrt(p_total / tau + d_total / sigma + 1e-6)
    move_out[...] = jnp.broadcast_to(moves, move_out.shape)
    pltpu.make_async_copy(primal_done, primal_out, out_sem.at[0]).wait()
    dual_copy.wait()


def shards(n_row, n_col, tiles, tile_row, tile_col, live_count, cost, upper, capacity, step_sizes, restart_flags):
    slots, width = tiles.shape[2], tiles.shape[3]
    p_rows, d_rows = cost.shape[0] // LANES, capacity.shape[0] // LANES
    p_share, n_z, n_line = p_rows // n_row, n_row // 2, int(n_col**0.5)
    f32, bf16, i32 = jnp.float32, jnp.bfloat16, jnp.int32
    hbm = pl.BlockSpec(memory_space=pltpu.HBM)
    anywhere = pl.BlockSpec(memory_space=pl.ANY)
    smem = pl.BlockSpec(memory_space=pltpu.SMEM)
    dma = pltpu.SemaphoreType.DMA
    out_shape = (
        jax.ShapeDtypeStruct((p_rows, LANES), f32),
        jax.ShapeDtypeStruct((d_rows, LANES), f32),
        jax.ShapeDtypeStruct((8, LANES), f32),
    )
    primal, dual, moves = pl.pallas_call(
        functools.partial(kernel, n_row, n_col),
        out_shape=out_shape,
        in_specs=[hbm] * 8 + [smem],
        out_specs=(anywhere, anywhere, pl.BlockSpec(memory_space=pltpu.VMEM)),
        scratch_shapes=[
            pltpu.VMEM((slots, width, width), bf16),
            pltpu.VMEM((slots, width, width), bf16),
            pltpu.VMEM((p_rows, LANES), f32),
            pltpu.VMEM((p_rows, LANES), f32),
            pltpu.VMEM((p_rows, LANES), f32),
            pltpu.VMEM((p_rows, LANES), f32),
            pltpu.VMEM((d_rows, LANES), f32),
            pltpu.VMEM((1, slots), i32),
            pltpu.VMEM((1, slots), i32),
            pltpu.SMEM((2,), f32),
            pltpu.SMEM((ITERS,), i32),
            pltpu.VMEM((p_rows // 2, 3 * slots), bf16),
            pltpu.VMEM((slots, p_rows // 2), bf16),
            pltpu.VMEM((d_rows // 2, 3 * slots), bf16),
            pltpu.VMEM((slots, d_rows // 2), bf16),
            pltpu.VMEM((p_rows, LANES), f32),
            pltpu.VMEM((p_rows, LANES), f32),
            pltpu.VMEM((d_rows, LANES), f32),
            pltpu.VMEM((d_rows, LANES), f32),
            pltpu.VMEM((p_rows, LANES), f32),
            pltpu.VMEM((d_rows, LANES), f32),
            pltpu.VMEM((slots, width), bf16),
            pltpu.VMEM((slots, width), f32),
            pltpu.VMEM((ITERS, p_rows, LANES), f32),
            pltpu.VMEM((ITERS, p_rows // 2, LANES), f32),
            pltpu.VMEM((ITERS, p_rows // 2, LANES), f32),
            pltpu.VMEM((ITERS, n_z - 1, p_share, LANES), f32),
            pltpu.VMEM((ITERS, p_rows, LANES), f32),
            pltpu.VMEM((ITERS, 2, n_line, d_rows // 2, LANES), f32),
            pltpu.VMEM((ITERS, 2, n_line, d_rows // 2, LANES), f32),
            pltpu.VMEM((8, LANES), f32),
            pltpu.VMEM((8, LANES), f32),
            pltpu.VMEM((n_col, 8, LANES), f32),
            pltpu.VMEM((n_row, 8, LANES), f32),
            dma((slots // GROUP,)), dma((7,)), dma((2,)),
            dma((ITERS,)), dma((ITERS, n_z)), dma((ITERS,)), dma((ITERS,)),
            dma((ITERS,)), dma((ITERS, n_z)), dma((ITERS,)), dma((ITERS,)),
            dma((ITERS,)), dma((ITERS, 2)), dma((ITERS, 2)), dma((2,)), dma((2,)),
        ],
        compiler_params=pltpu.CompilerParams(
            collective_id=0, has_side_effects=True, vmem_limit_bytes=VMEM_LIMIT
        ),
        name="pdhg",
    )(
        *(
            pltpu.with_memory_space_constraint(operand, pltpu.HBM)
            for operand in (
                tiles.reshape(slots, width, width),
                tile_col.reshape(1, slots),
                tile_row.reshape(1, slots),
                cost.reshape(p_rows, LANES),
                upper.reshape(p_rows, LANES),
                capacity.reshape(d_rows, LANES),
                step_sizes,
                restart_flags,
            )
        ),
        live_count,
    )
    return primal.reshape(-1), dual.reshape(-1), moves[:ITERS, 0]


def solution(mesh):
    in_specs = (
        P("row", "col", None, None, None),
        P("row", "col", None),
        P("row", "col", None),
        P("row", "col"),
        P("col"),
        P("col"),
        P("row"),
        P(),
        P(),
    )
    out_specs = (P("col"), P("row"), P())
    body = functools.partial(shards, mesh.shape["row"], mesh.shape["col"])
    return jax.shard_map(body, mesh=mesh, in_specs=in_specs, out_specs=out_specs, check_vma=False)
```

```python
import functools

import jax
import jax.numpy as jnp
from jax import lax
from jax.experimental import pallas as pl
from jax.experimental.pallas import tpu as pltpu
from jax.sharding import PartitionSpec as P

ITERS = 4
LANES = 128
GROUP = 16
VMEM_LIMIT = 48 * 2**20
MESH = pl.DeviceIdType.MESH


def split(values):
    high = values.astype(jnp.bfloat16)
    rest = values - high.astype(jnp.float32)
    mid = rest.astype(jnp.bfloat16)
    low = (rest - mid.astype(jnp.float32)).astype(jnp.bfloat16)
    return jnp.concatenate([high, mid, low], axis=0)


def kernel(
    n_row, n_col,
    tiles_hbm, col_hbm, row_hbm, cost_hbm, upper_hbm, cap_hbm, step_hbm, flag_hbm, count_ref,
    primal_out, dual_out, move_out,
    tiles, tiles_t, cost_in, upper_in, cost, upper, cap, col_index, row_index, step_ref, flag_ref,
    col_table, col_pick, row_table, row_pick,
    primal, sum_primal, dual, sum_dual, primal_done, dual_done, picked, terms,
    grad, pair_in, pair_sum, ring_in, primal_new, x_in, y_in,
    primal_sq, dual_sq, primal_sq_in, dual_sq_in,
    tile_sem, in_sem, out_sem,
    pair_send, pair_recv, ring_send, ring_recv, gather_send, gather_recv, pass_send, pass_recv,
    line_send, x_recv, y_recv, sq_send, sq_recv,
):
    r = lax.axis_index("row")
    c = lax.axis_index("col")
    z, core = lax.div(r, 2), lax.rem(r, 2)
    n_z, n_line = n_row // 2, int(n_col**0.5)
    x, y = lax.div(c, n_line), lax.rem(c, n_line)
    slots, width = tiles.shape[0], tiles.shape[1]
    p_rows, d_rows = primal.shape[0], dual.shape[0]
    p_half, p_share, d_half = p_rows // 2, p_rows // n_row, d_rows // 2
    groups = slots // GROUP
    other = 1 - core
    sibling = (2 * z + other, c)

    def tile_copy(g):
        part = pl.ds(g * GROUP, GROUP)
        return pltpu.make_async_copy(tiles_hbm.at[part], tiles.at[part], tile_sem.at[g])

    in_copies = [
        pltpu.make_async_copy(src, dst, in_sem.at[i])
        for i, (src, dst) in enumerate((
            (col_hbm, col_index), (row_hbm, row_index), (step_hbm, step_ref),
            (flag_hbm, flag_ref), (cost_hbm, cost_in), (upper_hbm, upper_in), (cap_hbm, cap),
        ))
    ]
    for copy in in_copies:
        copy.start()
    for g in range(groups):
        tile_copy(g).start()

    barrier = pltpu.get_barrier_semaphore()
    def greet(me, n, device):
        def one(i, _):
            to = device(lax.rem(me + 1 + i, n))
            pl.semaphore_signal(barrier, inc=1, device_id=to, device_id_type=MESH)
            return 0

        lax.fori_loop(0, n - 1, one, 0)

    greet(r, n_row, lambda to: (to, c))
    greet(c, n_col, lambda to: (r, to))

    for ref in (primal_sq, dual_sq):
        ref[...] = jnp.zeros_like(ref)
    for copy in in_copies:
        copy.wait()

    lane = lax.broadcasted_iota(jnp.int32, (1, 3 * slots), 1)
    live = lax.rem(lane, slots) < count_ref[0, 0]

    def tables(index_ref, n_blocks, table, pick):
        index = index_ref[...]
        key = jnp.where(live, jnp.concatenate([index, index, index], axis=1), -1)
        hot = jnp.where(lax.broadcasted_iota(jnp.int32, (n_blocks, 3 * slots), 0) == key, 1.0, 0.0)
        table[...] = hot.astype(jnp.bfloat16)
        pick[...] = hot[:, :slots].T.astype(jnp.bfloat16)

    tables(row_index, d_half, row_table, row_pick)
    tables(col_index, p_half, col_table, col_pick)
    tau, sigma = step_ref[0], step_ref[1]

    def deal(ref, rows):
        return ref[pl.ds(0, rows, stride=2), :], ref[pl.ds(1, rows, stride=2), :]

    def weave(ref, out):
        rows = ref.shape[0] // 2
        out[pl.ds(0, rows, stride=2), :] = ref[:rows]
        out[pl.ds(1, rows, stride=2), :] = ref[rows:]

    for dealt, ref in ((cost, cost_in), (upper, upper_in)):
        dealt[:p_half], dealt[p_half:] = deal(ref, p_half)
    capacity = jnp.concatenate(deal(cap, d_half), axis=0)

    def half_lanes(h):
        return pl.ds(pl.multiple_of(h * LANES, LANES), LANES)

    def pick_blocks(pick, values, h):
        chosen = jnp.dot(pick[...], values.astype(jnp.bfloat16), preferred_element_type=jnp.float32)
        picked[:, half_lanes(h)] = chosen.astype(jnp.bfloat16)

    def diagonal(values):
        depth = values.shape[1]
        at_row = lax.broadcasted_iota(jnp.int32, (GROUP, GROUP * depth), 0)
        at_tile = lax.div(lax.broadcasted_iota(jnp.int32, (GROUP, GROUP * depth), 1), depth)
        wide = jnp.concatenate([values] * GROUP, axis=1)
        return jnp.where(at_row == at_tile, wide, jnp.zeros((), jnp.bfloat16))

    def group_part(g):
        return pl.ds(g * GROUP, GROUP)

    def transposed_half(h):
        some = []
        for g in range(groups):
            part = group_part(g)
            right = tiles[part, :, half_lanes(h)].reshape(GROUP * width, LANES)
            some.append(jnp.dot(diagonal(picked[part, :]), right, preferred_element_type=jnp.float32))
        return jnp.dot(col_table[...], split(jnp.concatenate(some, axis=0)), preferred_element_type=jnp.float32)

    def forward_half(h, add):
        depth = pl.ds(pl.multiple_of(h * LANES, LANES), LANES)
        for g in range(groups):
            part = group_part(g)
            right = tiles_t[part, depth, :].reshape(GROUP * LANES, width)
            some = jnp.dot(diagonal(picked[part, half_lanes(h)]), right, preferred_element_type=jnp.float32)
            terms[part, :] = terms[part, :] + some if add else some

    def forward_early():
        at_row = lax.broadcasted_iota(jnp.int32, (GROUP, width), 0)

        def one(g, _):
            tile_copy(g).wait()
            part = pl.ds(pl.multiple_of(g * GROUP, GROUP), GROUP)
            mine = picked[part, :]
            total = jnp.zeros((GROUP, width), jnp.float32)
            for s in range(GROUP):
                left = jnp.where(at_row == s, mine, jnp.zeros((), jnp.bfloat16))
                total += lax.dot_general(
                    left, tiles[g * GROUP + s], (((1,), (1,)), ((), ())), preferred_element_type=jnp.float32
                )
            terms[part, :] = total
            return 0

        lax.fori_loop(0, groups, one, 0)

    def transpose_tiles(begin, end):
        def four(i, _):
            for s in range(4):
                tiles_t[4 * i + s] = tiles[4 * i + s].T
            return 0

        lax.fori_loop(begin // 4, end // 4, four, 0)

    def half_part(h):
        return pl.ds(pl.multiple_of(h * p_half, 8), p_half)

    def z_part(which_z):
        return pl.ds(pl.multiple_of(which_z * p_share, 8), p_share)

    def p_part(h, which_z):
        return pl.ds(pl.multiple_of(h * p_half + which_z * p_share, 8), p_share)

    def remote(src, dst, send, recv, device):
        return pltpu.make_async_remote_copy(
            src_ref=src, dst_ref=dst, send_sem=send, recv_sem=recv, device_id=device, device_id_type=MESH
        )

    z_to = [lax.rem(z + o, n_z) for o in range(n_z)]
    z_peers = [(2 * to + core, c) for to in z_to]
    near_first = sorted(range(1, n_z), key=lambda o: min(o, n_z - o))
    far_first = near_first[::-1]
    own_p = p_part(core, z)
    far_on_line = sorted(range(1, n_line), key=lambda o: -min(o, n_line - o))
    x_peers = [(r, lax.rem(x + o, n_line) * n_line + y) for o in far_on_line]
    y_peers = [(r, x * n_line + lax.rem(y + o, n_line)) for o in far_on_line]

    def sum_lines(ref, k, phase):
        total = ref[k, phase, 0]
        for i in range(1, n_line):
            total += ref[k, phase, i]
        return total

    def start_x(k, phase):
        for peer in x_peers:
            remote(x_in.at[k, phase, x], x_in.at[k, phase, x], line_send.at[k], x_recv.at[k, phase], peer).start()

    def start_y(k, phase):
        for peer in y_peers:
            remote(y_in.at[k, phase, y], y_in.at[k, phase, y], line_send.at[k], y_recv.at[k, phase], peer).start()

    def wait_line(ref, sem, k, phase):
        part = ref.at[k, phase, pl.ds(0, n_line - 1)]
        remote(part, part, line_send.at[k], sem.at[k, phase], sibling).wait_recv()

    def send_squares(ref, ref_in, w, me, n, device):
        ref_in[me] = ref[...]

        def one(i, _):
            to = lax.rem(me + n // 2 + i, n)
            remote(ref, ref_in.at[me], sq_send.at[w], sq_recv.at[w], device(to)).start()
            return 0

        lax.fori_loop(0, n // 2, one, 0)
        lax.fori_loop(n // 2 + 1, n, one, 0)

    def gradient_step(k):
        both = jnp.concatenate([dual[:d_half], dual[d_half:]], axis=1).astype(jnp.bfloat16)
        picked[...] = jnp.dot(row_pick[...], both, preferred_element_type=jnp.float32).astype(jnp.bfloat16)
        grad[k, half_part(other)] = transposed_half(other)
        pair = {}
        for o in far_first + [0]:
            to_z = z_to[o]
            pair[o] = remote(
                grad.at[k, p_part(other, to_z)], pair_in.at[k, z_part(to_z)],
                pair_send.at[k], pair_recv.at[k, o], sibling,
            )
            pair[o].start()
        grad[k, half_part(core)] = transposed_half(core)
        for o in far_first:
            to_z = z_to[o]
            pair[o].wait_recv()
            pair_sum[k, z_part(to_z)] = grad[k, p_part(core, to_z)] + pair_in[k, z_part(to_z)]
            remote(
                pair_sum.at[k, z_part(to_z)], ring_in.at[k, o - 1], ring_send.at[k], ring_recv.at[k], z_peers[o]
            ).start()
        pair[0].wait_recv()
        gradient = grad[k, own_p] + pair_in[k, z_part(z)]
        remote(ring_in.at[k], ring_in.at[k], ring_send.at[k], ring_recv.at[k], sibling).wait_recv()
        for i in range(n_z - 1):
            gradient += ring_in[k, i]

        primal_new[k, own_p] = jnp.clip(primal[own_p] - tau * (cost[own_p] + gradient), 0.0, upper[own_p])
        mine = primal_new.at[k, own_p]
        for o in far_first:
            remote(mine, mine, gather_send.at[k], gather_recv.at[k, o], z_peers[o]).start()
        remote(mine, mine, pass_send.at[k], pass_recv.at[k], sibling).start()
        for o in near_first:
            here = primal_new.at[k, p_part(core, z_to[n_z - o])]
            remote(here, here, gather_send.at[k], gather_recv.at[k, o], sibling).wait_recv()
            remote(here, here, pass_send.at[k], pass_recv.at[k], sibling).start()

    def extrapolated(k, h):
        return 2.0 * primal_new[k, half_part(h)] - primal[half_part(h)]

    def forward(k):
        pick_blocks(col_pick, extrapolated(k, core), core)
        forward_half(core, False)
        passed = primal_new.at[k, half_part(core)]
        remote(passed, passed, pass_send.at[k], pass_recv.at[k], sibling).wait_recv()
        pick_blocks(col_pick, extrapolated(k, other), other)
        forward_half(other, True)

    def load_step(k, counter, begin):
        x_in[k, 0, x] = jnp.dot(row_table[...], split(terms[:, :LANES]), preferred_element_type=jnp.float32)
        start_x(k, 0)
        y_in[k, 0, y] = jnp.dot(row_table[...], split(terms[:, LANES:]), preferred_element_type=jnp.float32)
        start_y(k, 0)

        counter = counter + 1.0
        flag = jnp.where(flag_ref[k] == 1, 1.0, 0.0)
        fresh = primal_new[k]
        step = fresh - primal[...]
        if begin:
            transpose_tiles(0, slots // 2)
        primal_sq[pl.ds(k, 1), :] = jnp.sum(step * step, axis=0, keepdims=True)
        total = sum_primal[...] + fresh
        again = jnp.full((p_rows, LANES), flag) > 0.5
        primal[...] = jnp.where(again, total / jnp.full((p_rows, LANES), counter), fresh)
        sum_primal[...] = jnp.where(again, 0.0, total)

        wait_line(x_in, x_recv, k, 0)
        y_in[k, 1, y] = sum_lines(x_in, k, 0)
        start_y(k, 1)
        wait_line(y_in, y_recv, k, 0)
        x_in[k, 1, x] = sum_lines(y_in, k, 0)
        start_x(k, 1)
        if begin:
            transpose_tiles(slots // 2, slots)

        @pl.when(k == ITERS - 1)
        def _():
            send_squares(primal_sq, primal_sq_in, 1, c, n_col, lambda to: (r, to))
            weave(primal, primal_done)
            pltpu.make_async_copy(primal_done, primal_out, out_sem.at[0]).start()

        wait_line(y_in, y_recv, k, 1)
        wait_line(x_in, x_recv, k, 1)
        loaded = jnp.concatenate([sum_lines(y_in, k, 1), sum_lines(x_in, k, 1)], axis=0)
        old = dual[...]
        fresh = jnp.maximum(old + sigma * (loaded - capacity), 0.0)
        step = fresh - old
        dual_sq[pl.ds(k, 1), :] = jnp.sum(step * step, axis=0, keepdims=True)

        @pl.when(k == ITERS - 1)
        def _():
            send_squares(dual_sq, dual_sq_in, 0, r, n_row, lambda to: (to, c))

        total = sum_dual[...] + fresh
        again = jnp.full((d_rows, LANES), flag) > 0.5
        dual[...] = jnp.where(again, total / jnp.full((d_rows, LANES), counter), fresh)
        sum_dual[...] = jnp.where(again, 0.0, total)
        return jnp.where(flag_ref[k] == 1, 0.0, counter)

    for ref in (primal, sum_primal, dual, sum_dual):
        ref[...] = jnp.zeros_like(ref)
    gradient_at_zero = 0.0
    primal_new[0] = jnp.clip(primal[...] - tau * (cost[...] + gradient_at_zero), 0.0, upper[...])
    for h in range(2):
        pick_blocks(col_pick, extrapolated(0, h), h)
    forward_early()
    pl.semaphore_wait(barrier, n_row - 1 + n_col - 1)
    counter = load_step(0, jnp.float32(0.0), True)

    def iteration(k, counter):
        gradient_step(k)
        forward(k)
        return load_step(k, counter, False)

    lax.fori_loop(1, ITERS, iteration, counter)

    weave(dual, dual_done)
    dual_copy = pltpu.make_async_copy(dual_done, dual_out, out_sem.at[1])
    dual_copy.start()

    def sent(k, _, begin=False):
        def wait(ref, sem):
            remote(ref, ref, sem.at[k], sem.at[k], sibling).wait_send()

        for _ in range(2):
            wait(x_in.at[k, 0, pl.ds(0, n_line - 1)], line_send)
            wait(y_in.at[k, 0, pl.ds(0, n_line - 1)], line_send)
        if begin:
            return 0
        wait(grad.at[k, pl.ds(0, n_z * p_share)], pair_send)
        wait(grad.at[k, pl.ds(0, (n_z - 1) * p_share)], ring_send)
        wait(grad.at[k, pl.ds(0, (n_z - 1) * p_share)], gather_send)
        wait(grad.at[k, pl.ds(0, n_z * p_share)], pass_send)
        return 0

    sent(0, 0, True)
    lax.fori_loop(1, ITERS, sent, 0)
    def squares(ref, i, n):
        part = ref.at[pl.ds(0, n - 1)]
        whole = remote(part, part, sq_send.at[i], sq_recv.at[i], sibling)
        whole.wait_send()
        whole.wait_recv()
        return jnp.sum(jnp.sum(ref[...], axis=0), axis=1, keepdims=True)

    p_total = squares(primal_sq_in, 1, n_col) / tau
    moves = jnp.sqrt(p_total + squares(dual_sq_in, 0, n_row) / sigma + 1e-6)
    move_out[...] = jnp.broadcast_to(moves, move_out.shape)
    pltpu.make_async_copy(primal_done, primal_out, out_sem.at[0]).wait()
    dual_copy.wait()


def shards(n_row, n_col, tiles, tile_row, tile_col, live_count, cost, upper, capacity, step_sizes, restart_flags):
    slots, width = tiles.shape[2], tiles.shape[3]
    p_rows, d_rows = cost.shape[0] // LANES, capacity.shape[0] // LANES
    p_share, n_z, n_line = p_rows // n_row, n_row // 2, int(n_col**0.5)
    f32, bf16, i32 = jnp.float32, jnp.bfloat16, jnp.int32
    hbm = pl.BlockSpec(memory_space=pltpu.HBM)
    anywhere = pl.BlockSpec(memory_space=pl.ANY)
    smem = pl.BlockSpec(memory_space=pltpu.SMEM)
    dma = pltpu.SemaphoreType.DMA
    out_shape = (
        jax.ShapeDtypeStruct((p_rows, LANES), f32),
        jax.ShapeDtypeStruct((d_rows, LANES), f32),
        jax.ShapeDtypeStruct((8, LANES), f32),
    )
    primal, dual, moves = pl.pallas_call(
        functools.partial(kernel, n_row, n_col),
        out_shape=out_shape,
        in_specs=[hbm] * 8 + [smem],
        out_specs=(anywhere, anywhere, pl.BlockSpec(memory_space=pltpu.VMEM)),
        scratch_shapes=[
            pltpu.VMEM((slots, width, width), bf16),
            pltpu.VMEM((slots, width, width), bf16),
            pltpu.VMEM((p_rows, LANES), f32),
            pltpu.VMEM((p_rows, LANES), f32),
            pltpu.VMEM((p_rows, LANES), f32),
            pltpu.VMEM((p_rows, LANES), f32),
            pltpu.VMEM((d_rows, LANES), f32),
            pltpu.VMEM((1, slots), i32),
            pltpu.VMEM((1, slots), i32),
            pltpu.SMEM((2,), f32),
            pltpu.SMEM((ITERS,), i32),
            pltpu.VMEM((p_rows // 2, 3 * slots), bf16),
            pltpu.VMEM((slots, p_rows // 2), bf16),
            pltpu.VMEM((d_rows // 2, 3 * slots), bf16),
            pltpu.VMEM((slots, d_rows // 2), bf16),
            pltpu.VMEM((p_rows, LANES), f32),
            pltpu.VMEM((p_rows, LANES), f32),
            pltpu.VMEM((d_rows, LANES), f32),
            pltpu.VMEM((d_rows, LANES), f32),
            pltpu.VMEM((p_rows, LANES), f32),
            pltpu.VMEM((d_rows, LANES), f32),
            pltpu.VMEM((slots, width), bf16),
            pltpu.VMEM((slots, width), f32),
            pltpu.VMEM((ITERS, p_rows, LANES), f32),
            pltpu.VMEM((ITERS, p_rows // 2, LANES), f32),
            pltpu.VMEM((ITERS, p_rows // 2, LANES), f32),
            pltpu.VMEM((ITERS, n_z - 1, p_share, LANES), f32),
            pltpu.VMEM((ITERS, p_rows, LANES), f32),
            pltpu.VMEM((ITERS, 2, n_line, d_rows // 2, LANES), f32),
            pltpu.VMEM((ITERS, 2, n_line, d_rows // 2, LANES), f32),
            pltpu.VMEM((8, LANES), f32),
            pltpu.VMEM((8, LANES), f32),
            pltpu.VMEM((n_col, 8, LANES), f32),
            pltpu.VMEM((n_row, 8, LANES), f32),
            dma((slots // GROUP,)), dma((7,)), dma((2,)),
            dma((ITERS,)), dma((ITERS, n_z)), dma((ITERS,)), dma((ITERS,)),
            dma((ITERS,)), dma((ITERS, n_z)), dma((ITERS,)), dma((ITERS,)),
            dma((ITERS,)), dma((ITERS, 2)), dma((ITERS, 2)), dma((2,)), dma((2,)),
        ],
        compiler_params=pltpu.CompilerParams(
            collective_id=0, has_side_effects=True, vmem_limit_bytes=VMEM_LIMIT
        ),
        name="pdhg",
    )(
        *(
            pltpu.with_memory_space_constraint(operand, pltpu.HBM)
            for operand in (
                tiles.reshape(slots, width, width),
                tile_col.reshape(1, slots),
                tile_row.reshape(1, slots),
                cost.reshape(p_rows, LANES),
                upper.reshape(p_rows, LANES),
                capacity.reshape(d_rows, LANES),
                step_sizes,
                restart_flags,
            )
        ),
        live_count,
    )
    return primal.reshape(-1), dual.reshape(-1), moves[:ITERS, 0]


def solution(mesh):
    in_specs = (
        P("row", "col", None, None, None),
        P("row", "col", None),
        P("row", "col", None),
        P("row", "col"),
        P("col"),
        P("col"),
        P("row"),
        P(),
        P(),
    )
    out_specs = (P("col"), P("row"), P())
    body = functools.partial(shards, mesh.shape["row"], mesh.shape["col"])
    return jax.shard_map(body, mesh=mesh, in_specs=in_specs, out_specs=out_specs, check_vma=False)
```

```python
import functools

import jax
import jax.numpy as jnp
from jax import lax
from jax.experimental import pallas as pl
from jax.experimental.pallas import tpu as pltpu
from jax.sharding import PartitionSpec as P

ITERS = 4
LANES = 128
GROUP = 32
VMEM_LIMIT = 48 * 2**20
MESH = pl.DeviceIdType.MESH


def split(values):
    high = values.astype(jnp.bfloat16)
    rest = values - high.astype(jnp.float32)
    mid = rest.astype(jnp.bfloat16)
    low = (rest - mid.astype(jnp.float32)).astype(jnp.bfloat16)
    return jnp.concatenate([high, mid, low], axis=0)


def kernel(
    n_row, n_col,
    tiles_hbm, col_hbm, row_hbm, cost_hbm, upper_hbm, cap_hbm, step_hbm, flag_hbm, count_ref,
    primal_out, dual_out, move_out,
    tiles, tiles_t, cost_in, upper_in, cost, upper, cap, col_index, row_index, step_ref, flag_ref,
    col_table, col_pick, row_table, row_pick,
    primal, sum_primal, dual, sum_dual, primal_done, dual_done, picked, terms,
    grad, pair_in, pair_sum, ring_in, primal_new, x_in, y_in,
    primal_sq, dual_sq, primal_sq_in, dual_sq_in,
    tile_sem, in_sem, out_sem,
    pair_send, pair_recv, ring_send, ring_recv, gather_send, gather_recv, pass_send, pass_recv,
    line_send, x_recv, y_recv, sq_send, sq_recv,
):
    r = lax.axis_index("row")
    c = lax.axis_index("col")
    z, core = lax.div(r, 2), lax.rem(r, 2)
    n_z, n_line = n_row // 2, int(n_col**0.5)
    x, y = lax.div(c, n_line), lax.rem(c, n_line)
    slots, width = tiles.shape[0], tiles.shape[1]
    p_rows, d_rows = primal.shape[0], dual.shape[0]
    p_half, p_share, d_half = p_rows // 2, p_rows // n_row, d_rows // 2
    groups = slots // GROUP
    other = 1 - core
    sibling = (2 * z + other, c)

    def tile_copy(g):
        part = pl.ds(g * GROUP, GROUP)
        return pltpu.make_async_copy(tiles_hbm.at[part], tiles.at[part], tile_sem.at[g])

    in_copies = [
        pltpu.make_async_copy(src, dst, in_sem.at[i])
        for i, (src, dst) in enumerate((
            (col_hbm, col_index), (row_hbm, row_index), (step_hbm, step_ref),
            (flag_hbm, flag_ref), (cost_hbm, cost_in), (upper_hbm, upper_in), (cap_hbm, cap),
        ))
    ]
    for copy in in_copies:
        copy.start()
    for g in range(groups):
        tile_copy(g).start()

    barrier = pltpu.get_barrier_semaphore()
    def greet(me, n, device):
        def one(i, _):
            to = device(lax.rem(me + 1 + i, n))
            pl.semaphore_signal(barrier, inc=1, device_id=to, device_id_type=MESH)
            return 0

        lax.fori_loop(0, n - 1, one, 0)

    greet(r, n_row, lambda to: (to, c))
    greet(c, n_col, lambda to: (r, to))

    for ref in (primal_sq, dual_sq):
        ref[...] = jnp.zeros_like(ref)
    for copy in in_copies:
        copy.wait()

    lane = lax.broadcasted_iota(jnp.int32, (1, 3 * slots), 1)
    live = lax.rem(lane, slots) < count_ref[0, 0]

    def tables(index_ref, n_blocks, table, pick):
        index = index_ref[...]
        key = jnp.where(live, jnp.concatenate([index, index, index], axis=1), -1)
        hot = jnp.where(lax.broadcasted_iota(jnp.int32, (n_blocks, 3 * slots), 0) == key, 1.0, 0.0)
        table[...] = hot.astype(jnp.bfloat16)
        pick[...] = hot[:, :slots].T.astype(jnp.bfloat16)

    tables(row_index, d_half, row_table, row_pick)
    tables(col_index, p_half, col_table, col_pick)
    tau, sigma = step_ref[0], step_ref[1]

    def deal(ref, rows):
        return ref[pl.ds(0, rows, stride=2), :], ref[pl.ds(1, rows, stride=2), :]

    def weave(ref, out):
        rows = ref.shape[0] // 2
        out[pl.ds(0, rows, stride=2), :] = ref[:rows]
        out[pl.ds(1, rows, stride=2), :] = ref[rows:]

    for dealt, ref in ((cost, cost_in), (upper, upper_in)):
        dealt[:p_half], dealt[p_half:] = deal(ref, p_half)
    capacity = jnp.concatenate(deal(cap, d_half), axis=0)

    def half_lanes(h):
        return pl.ds(pl.multiple_of(h * LANES, LANES), LANES)

    def pick_blocks(pick, values, h):
        chosen = jnp.dot(pick[...], values.astype(jnp.bfloat16), preferred_element_type=jnp.float32)
        picked[:, half_lanes(h)] = chosen.astype(jnp.bfloat16)

    def diagonal(values):
        depth = values.shape[1]
        at_row = lax.broadcasted_iota(jnp.int32, (GROUP, GROUP * depth), 0)
        at_tile = lax.div(lax.broadcasted_iota(jnp.int32, (GROUP, GROUP * depth), 1), depth)
        wide = jnp.concatenate([values] * GROUP, axis=1)
        return jnp.where(at_row == at_tile, wide, jnp.zeros((), jnp.bfloat16))

    def group_part(g):
        return pl.ds(g * GROUP, GROUP)

    def transposed_half(h):
        some = []
        for g in range(groups):
            part = group_part(g)
            right = tiles[part, :, half_lanes(h)].reshape(GROUP * width, LANES)
            some.append(jnp.dot(diagonal(picked[part, :]), right, preferred_element_type=jnp.float32))
        return jnp.dot(col_table[...], split(jnp.concatenate(some, axis=0)), preferred_element_type=jnp.float32)

    def forward_half(h, add):
        depth = pl.ds(pl.multiple_of(h * LANES, LANES), LANES)
        for g in range(groups):
            part = group_part(g)
            right = tiles_t[part, depth, :].reshape(GROUP * LANES, width)
            some = jnp.dot(diagonal(picked[part, half_lanes(h)]), right, preferred_element_type=jnp.float32)
            terms[part, :] = terms[part, :] + some if add else some

    def forward_early():
        at_row = lax.broadcasted_iota(jnp.int32, (GROUP, width), 0)

        def one(g, _):
            tile_copy(g).wait()
            part = pl.ds(pl.multiple_of(g * GROUP, GROUP), GROUP)
            mine = picked[part, :]
            total = jnp.zeros((GROUP, width), jnp.float32)
            for s in range(GROUP):
                left = jnp.where(at_row == s, mine, jnp.zeros((), jnp.bfloat16))
                total += lax.dot_general(
                    left, tiles[g * GROUP + s], (((1,), (1,)), ((), ())), preferred_element_type=jnp.float32
                )
            terms[part, :] = total
            return 0

        lax.fori_loop(0, groups, one, 0)

    def transpose_tiles(begin, end):
        def four(i, _):
            for s in range(4):
                tiles_t[4 * i + s] = tiles[4 * i + s].T
            return 0

        lax.fori_loop(begin // 4, end // 4, four, 0)

    def half_part(h):
        return pl.ds(pl.multiple_of(h * p_half, 8), p_half)

    def z_part(which_z):
        return pl.ds(pl.multiple_of(which_z * p_share, 8), p_share)

    def p_part(h, which_z):
        return pl.ds(pl.multiple_of(h * p_half + which_z * p_share, 8), p_share)

    def remote(src, dst, send, recv, device):
        return pltpu.make_async_remote_copy(
            src_ref=src, dst_ref=dst, send_sem=send, recv_sem=recv, device_id=device, device_id_type=MESH
        )

    z_to = [lax.rem(z + o, n_z) for o in range(n_z)]
    z_peers = [(2 * to + core, c) for to in z_to]
    near_first = sorted(range(1, n_z), key=lambda o: min(o, n_z - o))
    far_first = near_first[::-1]
    own_p = p_part(core, z)
    far_on_line = sorted(range(1, n_line), key=lambda o: -min(o, n_line - o))
    x_peers = [(r, lax.rem(x + o, n_line) * n_line + y) for o in far_on_line]
    y_peers = [(r, x * n_line + lax.rem(y + o, n_line)) for o in far_on_line]

    def sum_lines(ref, k, phase):
        total = ref[k, phase, 0]
        for i in range(1, n_line):
            total += ref[k, phase, i]
        return total

    def start_x(k, phase):
        for peer in x_peers:
            remote(x_in.at[k, phase, x], x_in.at[k, phase, x], line_send.at[k], x_recv.at[k, phase], peer).start()

    def start_y(k, phase):
        for peer in y_peers:
            remote(y_in.at[k, phase, y], y_in.at[k, phase, y], line_send.at[k], y_recv.at[k, phase], peer).start()

    def wait_line(ref, sem, k, phase):
        part = ref.at[k, phase, pl.ds(0, n_line - 1)]
        remote(part, part, line_send.at[k], sem.at[k, phase], sibling).wait_recv()

    def send_squares(ref, ref_in, w, me, n, device):
        ref_in[me] = ref[...]

        def one(i, _):
            to = lax.rem(me + n // 2 + i, n)
            remote(ref, ref_in.at[me], sq_send.at[w], sq_recv.at[w], device(to)).start()
            return 0

        lax.fori_loop(0, n // 2, one, 0)
        lax.fori_loop(n // 2 + 1, n, one, 0)

    def gradient_step(k):
        both = jnp.concatenate([dual[:d_half], dual[d_half:]], axis=1).astype(jnp.bfloat16)
        picked[...] = jnp.dot(row_pick[...], both, preferred_element_type=jnp.float32).astype(jnp.bfloat16)
        grad[k, half_part(other)] = transposed_half(other)
        pair = {}
        for o in far_first + [0]:
            to_z = z_to[o]
            pair[o] = remote(
                grad.at[k, p_part(other, to_z)], pair_in.at[k, z_part(to_z)],
                pair_send.at[k], pair_recv.at[k, o], sibling,
            )
            pair[o].start()
        grad[k, half_part(core)] = transposed_half(core)
        for o in far_first:
            to_z = z_to[o]
            pair[o].wait_recv()
            pair_sum[k, z_part(to_z)] = grad[k, p_part(core, to_z)] + pair_in[k, z_part(to_z)]
            remote(
                pair_sum.at[k, z_part(to_z)], ring_in.at[k, o - 1], ring_send.at[k], ring_recv.at[k], z_peers[o]
            ).start()
        pair[0].wait_recv()
        gradient = grad[k, own_p] + pair_in[k, z_part(z)]
        remote(ring_in.at[k], ring_in.at[k], ring_send.at[k], ring_recv.at[k], sibling).wait_recv()
        for i in range(n_z - 1):
            gradient += ring_in[k, i]

        primal_new[k, own_p] = jnp.clip(primal[own_p] - tau * (cost[own_p] + gradient), 0.0, upper[own_p])
        mine = primal_new.at[k, own_p]
        for o in far_first:
            remote(mine, mine, gather_send.at[k], gather_recv.at[k, o], z_peers[o]).start()
        remote(mine, mine, pass_send.at[k], pass_recv.at[k], sibling).start()
        for o in near_first:
            here = primal_new.at[k, p_part(core, z_to[n_z - o])]
            remote(here, here, gather_send.at[k], gather_recv.at[k, o], sibling).wait_recv()
            remote(here, here, pass_send.at[k], pass_recv.at[k], sibling).start()

    def extrapolated(k, h):
        return 2.0 * primal_new[k, half_part(h)] - primal[half_part(h)]

    def forward(k):
        pick_blocks(col_pick, extrapolated(k, core), core)
        forward_half(core, False)
        passed = primal_new.at[k, half_part(core)]
        remote(passed, passed, pass_send.at[k], pass_recv.at[k], sibling).wait_recv()
        pick_blocks(col_pick, extrapolated(k, other), other)
        forward_half(other, True)

    def load_step(k, counter, begin):
        x_in[k, 0, x] = jnp.dot(row_table[...], split(terms[:, :LANES]), preferred_element_type=jnp.float32)
        y_in[k, 0, y] = jnp.dot(row_table[...], split(terms[:, LANES:]), preferred_element_type=jnp.float32)
        start_x(k, 0)
        start_y(k, 0)

        counter = counter + 1.0
        flag = jnp.where(flag_ref[k] == 1, 1.0, 0.0)
        fresh = primal_new[k]
        step = fresh - primal[...]
        if begin:
            transpose_tiles(0, slots // 2)
        primal_sq[pl.ds(k, 1), :] = jnp.sum(step * step, axis=0, keepdims=True)
        total = sum_primal[...] + fresh
        again = jnp.full((p_rows, LANES), flag) > 0.5
        primal[...] = jnp.where(again, total / jnp.full((p_rows, LANES), counter), fresh)
        sum_primal[...] = jnp.where(again, 0.0, total)

        wait_line(x_in, x_recv, k, 0)
        y_in[k, 1, y] = sum_lines(x_in, k, 0)
        start_y(k, 1)
        wait_line(y_in, y_recv, k, 0)
        x_in[k, 1, x] = sum_lines(y_in, k, 0)
        start_x(k, 1)
        if begin:
            transpose_tiles(slots // 2, slots)

        @pl.when(k == ITERS - 1)
        def _():
            send_squares(primal_sq, primal_sq_in, 1, c, n_col, lambda to: (r, to))
            weave(primal, primal_done)
            pltpu.make_async_copy(primal_done, primal_out, out_sem.at[0]).start()

        wait_line(y_in, y_recv, k, 1)
        wait_line(x_in, x_recv, k, 1)
        loaded = jnp.concatenate([sum_lines(y_in, k, 1), sum_lines(x_in, k, 1)], axis=0)
        old = dual[...]
        fresh = jnp.maximum(old + sigma * (loaded - capacity), 0.0)
        step = fresh - old
        dual_sq[pl.ds(k, 1), :] = jnp.sum(step * step, axis=0, keepdims=True)

        @pl.when(k == ITERS - 1)
        def _():
            send_squares(dual_sq, dual_sq_in, 0, r, n_row, lambda to: (to, c))

        total = sum_dual[...] + fresh
        again = jnp.full((d_rows, LANES), flag) > 0.5
        dual[...] = jnp.where(again, total / jnp.full((d_rows, LANES), counter), fresh)
        sum_dual[...] = jnp.where(again, 0.0, total)
        return jnp.where(flag_ref[k] == 1, 0.0, counter)

    for ref in (primal, sum_primal, dual, sum_dual):
        ref[...] = jnp.zeros_like(ref)
    gradient_at_zero = 0.0
    primal_new[0] = jnp.clip(primal[...] - tau * (cost[...] + gradient_at_zero), 0.0, upper[...])
    for h in range(2):
        pick_blocks(col_pick, extrapolated(0, h), h)
    forward_early()
    pl.semaphore_wait(barrier, n_row - 1 + n_col - 1)
    counter = load_step(0, jnp.float32(0.0), True)

    def iteration(k, counter):
        gradient_step(k)
        forward(k)
        return load_step(k, counter, False)

    lax.fori_loop(1, ITERS, iteration, counter)

    weave(dual, dual_done)
    dual_copy = pltpu.make_async_copy(dual_done, dual_out, out_sem.at[1])
    dual_copy.start()

    def sent(k, _, begin=False):
        def wait(ref, sem):
            remote(ref, ref, sem.at[k], sem.at[k], sibling).wait_send()

        for _ in range(2):
            wait(x_in.at[k, 0, pl.ds(0, n_line - 1)], line_send)
            wait(y_in.at[k, 0, pl.ds(0, n_line - 1)], line_send)
        if begin:
            return 0
        wait(grad.at[k, pl.ds(0, n_z * p_share)], pair_send)
        wait(grad.at[k, pl.ds(0, (n_z - 1) * p_share)], ring_send)
        wait(grad.at[k, pl.ds(0, (n_z - 1) * p_share)], gather_send)
        wait(grad.at[k, pl.ds(0, n_z * p_share)], pass_send)
        return 0

    sent(0, 0, True)
    lax.fori_loop(1, ITERS, sent, 0)
    def squares(ref, i, n):
        part = ref.at[pl.ds(0, n - 1)]
        whole = remote(part, part, sq_send.at[i], sq_recv.at[i], sibling)
        whole.wait_send()
        whole.wait_recv()
        return jnp.sum(jnp.sum(ref[...], axis=0), axis=1, keepdims=True)

    p_total = squares(primal_sq_in, 1, n_col) / tau
    moves = jnp.sqrt(p_total + squares(dual_sq_in, 0, n_row) / sigma + 1e-6)
    move_out[...] = jnp.broadcast_to(moves, move_out.shape)
    pltpu.make_async_copy(primal_done, primal_out, out_sem.at[0]).wait()
    dual_copy.wait()


def shards(n_row, n_col, tiles, tile_row, tile_col, live_count, cost, upper, capacity, step_sizes, restart_flags):
    slots, width = tiles.shape[2], tiles.shape[3]
    p_rows, d_rows = cost.shape[0] // LANES, capacity.shape[0] // LANES
    p_share, n_z, n_line = p_rows // n_row, n_row // 2, int(n_col**0.5)
    f32, bf16, i32 = jnp.float32, jnp.bfloat16, jnp.int32
    hbm = pl.BlockSpec(memory_space=pltpu.HBM)
    anywhere = pl.BlockSpec(memory_space=pl.ANY)
    smem = pl.BlockSpec(memory_space=pltpu.SMEM)
    dma = pltpu.SemaphoreType.DMA
    out_shape = (
        jax.ShapeDtypeStruct((p_rows, LANES), f32),
        jax.ShapeDtypeStruct((d_rows, LANES), f32),
        jax.ShapeDtypeStruct((8, LANES), f32),
    )
    primal, dual, moves = pl.pallas_call(
        functools.partial(kernel, n_row, n_col),
        out_shape=out_shape,
        in_specs=[hbm] * 8 + [smem],
        out_specs=(anywhere, anywhere, pl.BlockSpec(memory_space=pltpu.VMEM)),
        scratch_shapes=[
            pltpu.VMEM((slots, width, width), bf16),
            pltpu.VMEM((slots, width, width), bf16),
            pltpu.VMEM((p_rows, LANES), f32),
            pltpu.VMEM((p_rows, LANES), f32),
            pltpu.VMEM((p_rows, LANES), f32),
            pltpu.VMEM((p_rows, LANES), f32),
            pltpu.VMEM((d_rows, LANES), f32),
            pltpu.VMEM((1, slots), i32),
            pltpu.VMEM((1, slots), i32),
            pltpu.SMEM((2,), f32),
            pltpu.SMEM((ITERS,), i32),
            pltpu.VMEM((p_rows // 2, 3 * slots), bf16),
            pltpu.VMEM((slots, p_rows // 2), bf16),
            pltpu.VMEM((d_rows // 2, 3 * slots), bf16),
            pltpu.VMEM((slots, d_rows // 2), bf16),
            pltpu.VMEM((p_rows, LANES), f32),
            pltpu.VMEM((p_rows, LANES), f32),
            pltpu.VMEM((d_rows, LANES), f32),
            pltpu.VMEM((d_rows, LANES), f32),
            pltpu.VMEM((p_rows, LANES), f32),
            pltpu.VMEM((d_rows, LANES), f32),
            pltpu.VMEM((slots, width), bf16),
            pltpu.VMEM((slots, width), f32),
            pltpu.VMEM((ITERS, p_rows, LANES), f32),
            pltpu.VMEM((ITERS, p_rows // 2, LANES), f32),
            pltpu.VMEM((ITERS, p_rows // 2, LANES), f32),
            pltpu.VMEM((ITERS, n_z - 1, p_share, LANES), f32),
            pltpu.VMEM((ITERS, p_rows, LANES), f32),
            pltpu.VMEM((ITERS, 2, n_line, d_rows // 2, LANES), f32),
            pltpu.VMEM((ITERS, 2, n_line, d_rows // 2, LANES), f32),
            pltpu.VMEM((8, LANES), f32),
            pltpu.VMEM((8, LANES), f32),
            pltpu.VMEM((n_col, 8, LANES), f32),
            pltpu.VMEM((n_row, 8, LANES), f32),
            dma((slots // GROUP,)), dma((7,)), dma((2,)),
            dma((ITERS,)), dma((ITERS, n_z)), dma((ITERS,)), dma((ITERS,)),
            dma((ITERS,)), dma((ITERS, n_z)), dma((ITERS,)), dma((ITERS,)),
            dma((ITERS,)), dma((ITERS, 2)), dma((ITERS, 2)), dma((2,)), dma((2,)),
        ],
        compiler_params=pltpu.CompilerParams(
            collective_id=0, has_side_effects=True, vmem_limit_bytes=VMEM_LIMIT
        ),
        name="pdhg",
    )(
        *(
            pltpu.with_memory_space_constraint(operand, pltpu.HBM)
            for operand in (
                tiles.reshape(slots, width, width),
                tile_col.reshape(1, slots),
                tile_row.reshape(1, slots),
                cost.reshape(p_rows, LANES),
                upper.reshape(p_rows, LANES),
                capacity.reshape(d_rows, LANES),
                step_sizes,
                restart_flags,
            )
        ),
        live_count,
    )
    return primal.reshape(-1), dual.reshape(-1), moves[:ITERS, 0]


def solution(mesh):
    in_specs = (
        P("row", "col", None, None, None),
        P("row", "col", None),
        P("row", "col", None),
        P("row", "col"),
        P("col"),
        P("col"),
        P("row"),
        P(),
        P(),
    )
    out_specs = (P("col"), P("row"), P())
    body = functools.partial(shards, mesh.shape["row"], mesh.shape["col"])
    return jax.shard_map(body, mesh=mesh, in_specs=in_specs, out_specs=out_specs, check_vma=False)
```
